128 devices in a mesh: gx: 16 (over z, y_hi, core), gy: 8 (over x, y_lo).
Axes of the slice: x: 4, y: 4 (y_hi: 2, y_lo: 2; y = y_hi * 2 + y_lo), z: 4, core: 2. Of those that a mesh axis runs over, the one named last changes fastest.
Arguments:
- surf_depth: float32 [2048, 1024], P('gx', 'gy'), may hold values from 0.2 to 2
- surf_bed: float32 [2048, 1024], P('gx', 'gy'), may hold values from -3 to 3
- surf_conv: float32 [2048, 1024], P('gx', 'gy'), may hold values from 0.25 to 1
- wet_mask: int32 [2048, 1024], P('gx', 'gy'), may hold values 0 or 1
- surf_salt: float32 [2048, 1024], P('gx', 'gy'), may hold values from 0.5 to 1.5
- seabed_leak: float32 [2048, 1024], P('gx', 'gy'), may hold values from 0.25 to 2
- seabed_shift: int32 [16, 8, 128, 2], P('gx', 'gy'), may hold values from -32 to 32, as said below
- active_count: int32 [16, 8, 128], P('gx', 'gy'), may hold values from 0 to 128
- aq_head: float32 [96, 128, 1024], P(None, 'gx', 'gy'), may hold values from -4 to 4
- aq_salt: float32 [96, 128, 1024], P(None, 'gx', 'gy'), may hold values from 0 to 1
- aq_cond: float32 [96, 128, 1024], P(None, 'gx', 'gy'), may hold values from 0.25 to 4
Outputs:
- surf_out: float32 [2048, 1024], P('gx', 'gy')
- head_out: float32 [96, 128, 1024], P(None, 'gx', 'gy')
- salt_out: float32 [96, 128, 1024], P(None, 'gx', 'gy')
The draws below stay inside these ranges and needn't reach their ends.
Inputs may be any that keep to these rules, and one draw needn't show every extreme that they name: `seabed_shift`: component 0 is a shift by whole surface rows along the coast, both ends reached; component 1 is -1, 0 or 1 tiles inland.
All inputs are finite; a program needn't handle non-finite values. No bound on the sum of `wet_mask` on one device may be relied on, other than what follows from the above.
Results may differ from the reference program's by a relative error of at most 0.000076.
Values sent between devices are 32-bit elements; how exact they have to be, the bound alone decides.
No kernel may reach another device: no remote copies, remote signals or barrier semaphores. Data moves between devices by JAX's collectives and lax.ppermute only.
A program may use at most 256 MiB of HBM per device.

```python
import math
import jax
import jax.numpy as jnp

CELLS = 128
SX = 128
AX = 8
NL = 96
SURF_STEPS = 4
AQ_ITERS = 6
SHIFT = 32
SURF_X = 2048
SURF_Y = 1024
AQ_X = 128
AQ_Y = 1024
N_GX = 16
N_GY = 8


def draw_seabed_shift(key, part):
    along_key = jax.random.fold_in(key, 11)
    inland_key = jax.random.fold_in(key, 12)
    along = jax.random.randint(along_key, (N_GX, N_GY, SX), -SHIFT, SHIFT + 1, dtype=jnp.int32)
    along = along.at[0, 0, 0].set(SHIFT).at[0, 0, 1].set(-SHIFT)
    picked = jax.random.randint(inland_key, (N_GX, N_GY, SX), 0, 8, dtype=jnp.int32)
    inland = jnp.where(picked == 0, -1, jnp.where(picked == 1, 1, 0)).astype(jnp.int32)
    return jnp.stack([along, inland], axis=-1).astype(jnp.int32)


def with_ends(drawn, rng, least, largest):
    longest = drawn.shape.index(max(drawn.shape))
    spots = []
    for shift in (0, 1):
        where = [jax.random.randint(jax.random.fold_in(rng, axis), (), 0, length) for axis, length in enumerate(drawn.shape)]
        where[longest] = (where[longest] + shift) % drawn.shape[longest]
        spots.append(tuple(where))
    return drawn.at[spots[0]].set(least).at[spots[1]].set(largest)


def block_levels(key, shape, cuts, smallest, high):
    def one(position, parts):
        draws = jax.random.uniform(jax.random.fold_in(jax.random.fold_in(key, 6), position), (parts,), jnp.float32, smallest / len(cuts), high / len(cuts))
        return jnp.repeat(jnp.exp(draws), shape[position] // parts).reshape((-1,) + (1,) * (len(shape) - position - 1))

    level = one(*cuts[0])
    for cut in cuts[1:]:
        level = level * one(*cut)
    return level


def bell_draw(key, extent, scale, most, pieces=(), kind=jnp.bfloat16):
    level = block_levels(key, extent, pieces, -0.22, 0.18) if pieces else 1.0
    entries = jax.random.normal(key, extent, jnp.float32) * scale * level
    return jnp.minimum(jnp.maximum(entries, -most), most).astype(kind)


def setup_inputs(seed: int = 0) -> dict:
    seeds = jax.random.split(jax.random.key(seed), 12)
    surf_depth = jnp.clip(0.2 + 1.8 * jax.random.uniform(seeds[0], (SURF_X, SURF_Y), jnp.float32) ** block_levels(seeds[0], (SURF_X, SURF_Y), ((0, 16), (1, 8)), -0.2, 0.2), 0.2, 2.0)
    surf_bed = bell_draw(seeds[1], (SURF_X, SURF_Y), 0.5, 3.0, ((0, 16), (1, 8)), jnp.float32)
    surf_conv = jnp.clip(jnp.exp(math.log(1.0) - 1.3862944 * jax.random.uniform(seeds[2], (SURF_X, SURF_Y), jnp.float32) ** block_levels(seeds[2], (SURF_X, SURF_Y), ((0, 16), (1, 8)), -0.2, 0.2)), 0.25, 1.0)
    wet_mask = with_ends((jax.random.randint(seeds[3], (SURF_X, SURF_Y), 0, 4) < 3).astype(jnp.int32), jax.random.fold_in(seeds[3], 1), 0, 1)
    surf_salt = jnp.clip(0.5 + 1.0 * jax.random.uniform(seeds[4], (SURF_X, SURF_Y), jnp.float32) ** block_levels(seeds[4], (SURF_X, SURF_Y), ((0, 16), (1, 8)), -0.2, 0.2), 0.5, 1.5)
    seabed_leak = jnp.clip(jnp.exp(math.log(2.0) - 2.0794415 * jax.random.uniform(seeds[5], (SURF_X, SURF_Y), jnp.float32) ** block_levels(seeds[5], (SURF_X, SURF_Y), ((0, 16), (1, 8)), -0.2, 0.2)), 0.25, 2.0)
    seabed_shift = draw_seabed_shift(jax.random.fold_in(seeds[11], 71), 0)
    active_count = with_ends(jax.random.randint(seeds[7], (N_GX, N_GY, SX), 0, CELLS + 1), jax.random.fold_in(seeds[7], 1), 0, CELLS).astype(jnp.int32)
    aq_head = bell_draw(seeds[8], (NL, AQ_X, AQ_Y), 0.25, 4.0, ((1, 16), (2, 8)), jnp.float32)
    aq_salt = jnp.clip(1.0 * jax.random.uniform(seeds[9], (NL, AQ_X, AQ_Y), jnp.float32) ** block_levels(seeds[9], (NL, AQ_X, AQ_Y), ((1, 16), (2, 8)), -0.2, 0.2), 0.0, 1.0)
    aq_cond = jnp.clip(jnp.exp(math.log(4.0) - 2.7725887 * jax.random.uniform(seeds[10], (NL, AQ_X, AQ_Y), jnp.float32) ** block_levels(seeds[10], (NL, AQ_X, AQ_Y), ((1, 16), (2, 8)), -0.2, 0.2)), 0.25, 4.0)
    return {"surf_depth": surf_depth, "surf_bed": surf_bed, "surf_conv": surf_conv, "wet_mask": wet_mask, "surf_salt": surf_salt, "seabed_leak": seabed_leak, "seabed_shift": seabed_shift, "active_count": active_count, "aq_head": aq_head, "aq_salt": aq_salt, "aq_cond": aq_cond}


surface_rate = 0.24
time_step = 0.05
density_slope = 0.025
porosity = 0.35
spread_side = 0.1
spread_vertical = 0.1

def surface_flux(level_pad, conduct_pad):
    water_level = level_pad[1:-1, 1:-1]
    conduct = conduct_pad[1:-1, 1:-1]
    summed = conduct_pad[2:, 1:-1] * (level_pad[2:, 1:-1] - water_level)
    summed = summed + conduct_pad[:-2, 1:-1] * (level_pad[:-2, 1:-1] - water_level)
    summed = summed + conduct_pad[1:-1, 2:] * (level_pad[1:-1, 2:] - water_level)
    summed = summed + conduct_pad[1:-1, :-2] * (level_pad[1:-1, :-2] - water_level)
    return conduct * summed

def tridiagonal(sub_diag, main_diag, super_diag, source_term):
    layers = source_term.shape[0]
    prev_upper = jnp.zeros_like(source_term[0])
    prev_source = jnp.zeros_like(source_term[0])
    uppers = []
    sources = []
    for layer in range(layers):
        pivots = main_diag[layer] - sub_diag[layer] * prev_upper
        prev_upper = super_diag[layer] / pivots
        prev_source = (source_term[layer] - sub_diag[layer] * prev_source) / pivots
        uppers.append(prev_upper)
        sources.append(prev_source)
    following = jnp.zeros_like(source_term[0])
    solved = [following] * layers
    for layer in range(layers - 1, -1, -1):
        following = sources[layer] - uppers[layer] * following
        solved[layer] = following
    return jnp.stack(solved)

def aquifer_update(head_pad, salt_pad, rock_pad, vertical, seabed):
    head = head_pad[:, 1:-1, 1:-1]
    salt = salt_pad[:, 1:-1, 1:-1]
    rock = rock_pad[:, 1:-1, 1:-1]
    offsets = ((slice(2, None), slice(1, -1)), (slice(None, -2), slice(1, -1)), (slice(1, -1), slice(2, None)), (slice(1, -1), slice(None, -2)))
    side_flow = jnp.zeros_like(head)
    side_salt = jnp.zeros_like(head)
    for first_cut, second_cut in offsets:
        weights = rock * rock_pad[:, first_cut, second_cut]
        flux = weights * (head_pad[:, first_cut, second_cut] - head)
        neighbour_salt = salt_pad[:, first_cut, second_cut]
        side_flow = side_flow + flux
        side_salt = side_salt + (jnp.maximum(flux, 0.0) * neighbour_salt + jnp.minimum(flux, 0.0) * salt + spread_side * weights * (neighbour_salt - salt))
    leak_total, leak_level, leak_salt = seabed
    edge_zero = jnp.zeros_like(head[:1])
    mean_salt = 0.5 * (salt[:-1] + salt[1:])
    lifting = density_slope * vertical * mean_salt
    upper_link = jnp.concatenate([vertical, edge_zero], axis=0)
    lower_link = jnp.concatenate([edge_zero, vertical], axis=0)
    source_head = head + time_step * side_flow - jnp.concatenate([lifting, edge_zero], axis=0) + jnp.concatenate([edge_zero, lifting], axis=0)
    source_head = source_head.at[0].add(leak_level)
    middle = 1.0 + upper_link + lower_link
    middle = middle.at[0].add(leak_total)
    new_head = tridiagonal(-lower_link, middle, -upper_link, source_head)
    rising = vertical * (new_head[1:] - new_head[:-1]) - lifting
    carried = jnp.maximum(rising, 0.0) * salt[1:] + jnp.minimum(rising, 0.0) * salt[:-1]
    source_salt = porosity * salt + time_step * (side_salt + jnp.concatenate([carried, edge_zero], axis=0) - jnp.concatenate([edge_zero, carried], axis=0))
    source_salt = source_salt.at[0].add(leak_salt)
    salt_middle = porosity + spread_vertical * (upper_link + lower_link)
    salt_middle = salt_middle.at[0].add(leak_total)
    new_salt = tridiagonal(-spread_vertical * lower_link, salt_middle, -spread_vertical * upper_link, source_salt)
    return (new_head, new_salt)

def into_blocks(field):
    return field.reshape(N_GX, SX, N_GY, CELLS).transpose(0, 2, 1, 3)

def pad_sides(field):
    return jnp.pad(field, ((0, 0), (1, 1), (1, 1)))

def reference(surf_depth, surf_bed, surf_conv, wet_mask, surf_salt, seabed_leak, seabed_shift, active_count, aq_head, aq_salt, aq_cond):
    wet = wet_mask.astype(jnp.float32)
    conduct = wet * jnp.sqrt(surf_conv)
    water_level = surf_bed + surf_depth
    depth = surf_depth
    level_sum = jnp.zeros_like(depth)
    conduct_pad = jnp.pad(conduct, 1)
    for step_index in range(SURF_STEPS):
        moved = surface_rate * surface_flux(jnp.pad(water_level, 1), conduct_pad)
        depth = depth + moved
        water_level = water_level + moved
        level_sum = level_sum + water_level
    mean_level = level_sum / SURF_STEPS
    cell_index = jnp.arange(CELLS, dtype=jnp.int32)
    active = (cell_index[None, None, None, :] < active_count[..., None]).astype(jnp.float32)
    leak_cells = into_blocks(wet) * active * into_blocks(seabed_leak)
    leak_level = leak_cells * into_blocks(mean_level)
    leak_salt = leak_cells * into_blocks(surf_salt)
    along = seabed_shift[..., 0].astype(jnp.int32)
    inland = seabed_shift[..., 1].astype(jnp.int32)
    coast_index = jnp.arange(N_GX, dtype=jnp.int32)[:, None, None]
    inland_index = jnp.arange(N_GY, dtype=jnp.int32)[None, :, None]
    block_index = jnp.arange(SX, dtype=jnp.int32)[None, None, :]
    global_row = coast_index * SX + block_index + along
    aquifer_row = jnp.clip(jnp.floor_divide(global_row, SX // AX), 0, AX * N_GX - 1).astype(jnp.int32)
    tile = jnp.clip(inland_index + inland, 0, N_GY - 1).astype(jnp.int32)
    column_index = (tile * CELLS)[..., None] + cell_index
    row_index = jnp.broadcast_to(aquifer_row[..., None], column_index.shape)
    empty = jnp.zeros((AX * N_GX, CELLS * N_GY), jnp.float32)
    seabed = (empty.at[row_index, column_index].add(leak_cells), empty.at[row_index, column_index].add(leak_level), empty.at[row_index, column_index].add(leak_salt))
    rock_pad = pad_sides(jnp.sqrt(aq_cond))
    vertical = 2.0 * aq_cond[:-1] * aq_cond[1:] / (aq_cond[:-1] + aq_cond[1:])
    head, salt = (aq_head, aq_salt)
    for step_index in range(AQ_ITERS):
        head, salt = aquifer_update(pad_sides(head), pad_sides(salt), rock_pad, vertical, seabed)
    return (depth, head, salt)
```

```python
import functools

import jax
import jax.numpy as jnp
from jax import lax
from jax.experimental import pallas as pl
from jax.experimental.pallas import tpu as pltpu
from jax.sharding import PartitionSpec as P

SURF_STEPS = 4
AQ_ITERS = 6
HALO = 6

surface_rate = 0.24
time_step = 0.05
density_slope = 0.025
porosity = 0.35
spread_side = 0.1
spread_vertical = 0.1

F32 = jnp.float32
VMEM_LIMIT = 48 * 2**20


def shift(block, axis, step):
    count = lax.axis_size(axis)
    return lax.ppermute(block, axis, [(i, (i + step) % count) for i in range(count)])


def call(body, outs, args, name, scratch=(), keep=None):
    shapes = [
        jax.ShapeDtypeStruct(shape, F32) if keep is not None and i in keep else pltpu.VMEM(shape, F32)
        for i, shape in enumerate(outs)
    ]
    return pl.pallas_call(
        body,
        out_shape=shapes,
        in_specs=[pl.BlockSpec(memory_space=pltpu.VMEM)] * len(args),
        out_specs=[pl.BlockSpec(memory_space=pltpu.VMEM)] * len(outs),
        scratch_shapes=list(scratch),
        compiler_params=pltpu.CompilerParams(vmem_limit_bytes=VMEM_LIMIT),
        name=name,
    )(*args)


def lanes(shape):
    return lax.broadcasted_iota(jnp.int32, shape, len(shape) - 1)


def rows_of(shape):
    return lax.broadcasted_iota(jnp.int32, shape, len(shape) - 2)


def roll(x, by, axis):
    by = by % x.shape[axis]
    return x if by == 0 else pltpu.roll(x, by, axis)


def pack_lanes(tiles, lane):
    low = tiles[0]
    high = roll(tiles[0], 8, 1)
    for i in range(1, len(tiles)):
        here = lane >= 8 * i
        low = jnp.where(here, roll(tiles[i], 8 * i, 1), low)
        high = jnp.where(here, roll(tiles[i], 8 * i + 8, 1), high)
    return low, high


def pack_inland(head, salt, cond, depth, bed, conv, wet, to_low, to_high, rows_low, rows_high):
    lane = lanes((8, 128))
    sub = rows_of((8, 128))
    level_rows, conduct_rows, tiles = [], [], []
    for t in range(16):
        here = slice(8 * t, 8 * t + 8)
        level = bed[here, :] + depth[here, :]
        conduct = wet[here, :].astype(F32) * jnp.sqrt(conv[here, :])
        level_rows.append(level)
        conduct_rows.append(conduct)
        tiles.append((jnp.where(lane < 4, level, roll(conduct, 4, 1)), jnp.where(lane < 4, roll(level, 4, 1), roll(conduct, 8, 1))))
    low, high = tiles[0]
    for t in range(1, 16):
        here = lane >= 8 * t
        low = jnp.where(here, roll(tiles[t][0], 8 * t, 1), low)
        high = jnp.where(here, roll(tiles[t][1], 8 * t, 1), high)
    to_low[144:152, :] = low
    to_high[144:152, :] = high
    rows_low[...] = jnp.where(sub < 4, level_rows[0], roll(conduct_rows[0], 4, 0))
    rows_high[...] = jnp.where(sub >= 4, level_rows[15], roll(conduct_rows[15], 4, 0))
    for a, ref in enumerate((head, salt, cond)):
        def group(g, _, a=a, ref=ref):
            low, high = pack_lanes([ref[g * 16 + i] for i in range(16)], lane)
            at = pl.ds(pl.multiple_of((a * 6 + g) * 8, 8), 8)
            to_low[at, :] = low
            to_high[at, :] = high
            return 0

        lax.fori_loop(0, 6, group, 0)


def pack_coast(head, salt, cond, to_low, to_high):
    for a, ref in enumerate((head, salt, cond)):
        def group(g, _, a=a, ref=ref):
            for i in range(4):
                to_low[a * 24 + g, 6 * i : 6 * i + 6, :] = ref[4 * g + i, 0:6, :]
                to_high[a * 24 + g, 6 * i : 6 * i + 6, :] = ref[4 * g + i, 2:8, :]
            return 0

        lax.fori_loop(0, 24, group, 0)


def join_rims(right, left, rows_low, rows_high, to_low, to_high):
    for out, rows in ((to_low, rows_low), (to_high, rows_high)):
        out[0:152, :] = right[...]
        out[152:304, :] = left[...]
        out[304:312, :] = rows[...]


def inside(shape, row_low, row_high, col_low, col_high):
    gx, gy = lax.axis_index("gx"), lax.axis_index("gy")
    last_x, last_y = lax.axis_size("gx") - 1, lax.axis_size("gy") - 1
    one = jnp.ones(shape, F32)
    zero = jnp.zeros(shape, F32)
    has = lambda there: jnp.where(there, 1.0, 0.0).astype(F32)
    row = jnp.where(row_high, one * has(gx < last_x), jnp.where(row_low, one * has(gx > 0), one))
    lane = lanes(shape)
    col = jnp.where(
        lane < 128,
        one,
        jnp.where(
            lane < 128 + col_high,
            one * has(gy < last_y),
            jnp.where(lane >= 256 - col_low, one * has(gy > 0), zero),
        ),
    )
    return row * col


def dot(a, b, dims):
    return lax.dot_general(a, b, (dims, ((), ())), precision=lax.Precision.HIGHEST, preferred_element_type=F32)


def surface(depth, bed, conv, wet, salt, leak, shifts, counts, right, left, above, below, depth_out, to_low, to_high, to_low2, to_high2, own, level_ref, conduct_ref):
    lane = lanes((8, 128))
    sub = rows_of((8, 128))
    ring = lanes((8, 256))
    sub_ring = rows_of((8, 256))
    column_in = inside((8, 256), sub_ring < 0, sub_ring < 0, 4, 4)
    corner_in = inside((8, 256), sub_ring >= 4, sub_ring < 4, 4, 4)

    def sides(r, l, t):
        level = jnp.where(lane < 4, roll(r, -8 * t, 1), roll(l, 124 - 8 * t, 1))
        conduct = jnp.where(lane < 4, roll(r, -8 * t - 4, 1), roll(l, 120 - 8 * t, 1))
        return level, conduct

    r, l = right[144:152, :], left[144:152, :]
    for t in range(16):
        here = slice(8 * t, 8 * t + 8)
        level, conduct = sides(r, l, t)
        level_ref[here, 0:128] = bed[here, :] + depth[here, :]
        level_ref[here, 128:256] = level
        conduct_ref[here, 0:128] = wet[here, :].astype(F32) * jnp.sqrt(conv[here, :])
        conduct_ref[here, 128:256] = conduct * column_in[:, 128:]
    high_rows, low_rows = above[304:312, :], below[304:312, :]
    high_sides = sides(above[144:152, :], above[296:304, :], 0)
    low_sides = sides(below[144:152, :], below[296:304, :], 15)
    level_ref[128:136, 0:128] = jnp.where(sub < 4, high_rows, low_rows)
    level_ref[128:136, 128:256] = jnp.where(sub < 4, high_sides[0], low_sides[0])
    conduct_ref[128:136, 0:128] = roll(jnp.where(sub >= 4, high_rows, low_rows), 4, 0) * corner_in[:, :128]
    conduct_ref[128:136, 128:256] = jnp.where(sub < 4, high_sides[1], low_sides[1]) * corner_in[:, 128:]

    level = level_ref[...]
    conduct = conduct_ref[...]
    link_x = surface_rate * conduct * roll(conduct, -1, 0)
    link_y = surface_rate * conduct * roll(conduct, -1, 1)
    final = depth[...]
    total = jnp.zeros((128, 128), F32)
    for _ in range(SURF_STEPS):
        flow_x = link_x * (roll(level, -1, 0) - level)
        flow_y = link_y * (roll(level, -1, 1) - level)
        moved = (flow_x - roll(flow_x, 1, 0)) + (flow_y - roll(flow_y, 1, 1))
        level = level + moved
        final = final + moved[0:128, 0:128]
        total = total + level[0:128, 0:128]
    depth_out[...] = final
    mean_level = total * (1.0 / SURF_STEPS)

    square = (128, 128)
    count = jnp.transpose(jnp.broadcast_to(counts[...].astype(F32), square))
    active = jnp.where(lanes(square).astype(F32) < count, 1.0, 0.0)
    cells = wet[...].astype(F32) * active * leak[...]
    gx, gy = lax.axis_index("gx"), lax.axis_index("gy")
    last_row, last_tile = 8 * lax.axis_size("gx") - 1, lax.axis_size("gy") - 1
    block = rows_of((128, 1))
    global_row = gx * 128 + block + shifts[:, 0:1]
    row = jnp.clip(jnp.right_shift(global_row, 4), 0, last_row) - gx * 8 + 2
    tile = jnp.clip(gy + shifts[:, 1:2], 0, last_tile) - gy + 1
    target = tile * 16 + row
    choose = jnp.where(lanes((128, 128)) == target, 1.0, 0.0)
    choose = jnp.transpose(choose)[0:48]
    sums = [dot(choose, term, ((1,), (0,))) for term in (cells, cells * mean_level, cells * salt[...])]
    lane48 = lanes((16, 128))
    for i, total in enumerate(sums):
        at = slice(128 * i, 128 * i + 128)
        to_low[:, at] = total[0:32]
        to_high[:, at] = total[16:48]
        to_low2[:, at] = total[0:16]
        to_high2[:, at] = total[32:48]
        own[:, 256 * i : 256 * i + 128] = total[16:32]
        own[:, 256 * i + 128 : 256 * i + 256] = jnp.where(lane48 < 8, total[32:48], jnp.where(lane48 >= 120, total[0:16], 0.0))


def sum_inland(own, right, left, right2, left2, gathered, to_low, to_high):
    lane = lanes((16, 128))
    for i in range(3):
        at = slice(128 * i, 128 * i + 128)
        first = slice(256 * i, 256 * i + 128)
        second = slice(256 * i + 128, 256 * i + 256)
        here = own[:, first] + right[0:16, at] + left[16:32, at]
        beside = own[:, second] + jnp.where(
            lane < 8,
            right[16:32, at] + right2[:, at],
            jnp.where(lane >= 120, left[0:16, at] + left2[:, at], 0.0),
        )
        gathered[:, first] = here
        gathered[:, second] = beside
    to_low[...] = gathered[0:8, :]
    to_high[...] = gathered[4:12, :]


def up(t):
    s = rows_of(t[0].shape)
    r = [roll(x, -1, 0) for x in t]
    if len(t) == 2:
        return [jnp.where(s == 7, r[1], r[0]), jnp.where(s == 7, r[0], r[1])]
    return [
        jnp.where(s == 7, r[1], r[0]),
        jnp.where(s == 7, r[0], jnp.where(s == 3, roll(t[2], 3, 0), r[1])),
        jnp.where(s == 7, roll(t[1], 3, 0), r[2]),
    ]


def down(t):
    s = rows_of(t[0].shape)
    r = [roll(x, 1, 0) for x in t]
    if len(t) == 2:
        return [jnp.where(s == 0, r[1], r[0]), jnp.where(s == 0, r[0], r[1])]
    return [
        jnp.where(s == 0, r[1], r[0]),
        jnp.where(s == 0, r[0], jnp.where(s == 4, roll(t[2], 5, 0), r[1])),
        jnp.where(s == 0, roll(t[1], 5, 0), r[2]),
    ]


def nxt(t):
    return [roll(x, -1, 1) for x in t]


def prv(t):
    return [roll(x, 1, 1) for x in t]


def sides_of(h, c, wx, wy):
    flow = salt = None
    for w, ahead, back in ((wx, up, down), (wy, nxt, prv)):
        hs, cs = ahead(h), ahead(c)
        f, g = [], []
        for i in range(len(h)):
            dh = hs[i] - h[i]
            moved = dh * jnp.where(dh > 0, cs[i], c[i]) + spread_side * (cs[i] - c[i])
            f.append(w[i] * dh)
            g.append(w[i] * moved)
        fb, gb = back(f), back(g)
        f = [a - b for a, b in zip(f, fb)]
        g = [a - b for a, b in zip(g, gb)]
        flow = f if flow is None else [a + b for a, b in zip(flow, f)]
        salt = g if salt is None else [a + b for a, b in zip(salt, g)]
    return flow, salt


def aquifer(head, salt, cond, right, left, above, below, high, low, gathered, leak_high, leak_low, head_out, salt_out, hy, cz, kk, ss, wx, wy, vv, ip, uu, iq, leak):
    layers = head.shape[0]
    lane = lanes((8, 128))
    sub = rows_of((8, 128))

    never = rows_of((8, 256)) < 0
    s = rows_of((8, 256))
    one = inside((8, 256), never, never, HALO, HALO)
    masks = [
        one,
        inside((8, 256), s >= 4, s < 4, HALO, HALO),
        inside((8, 256), s >= 4, s < 4, HALO, HALO) * jnp.where((s < 2) | (s >= 6), 1.0, 0.0),
    ]

    for a, (ref, ext) in enumerate(((head, hy), (salt, cz), (cond, kk))):
        def group(g, _, a=a, ref=ref, ext=ext):
            at = pl.multiple_of((a * 6 + g) * 8, 8)
            r, l = right[pl.ds(at, 8), :], left[pl.ds(at, 8), :]
            rx = jnp.where(sub < 4, above[pl.ds(at, 8), :], below[pl.ds(at, 8), :])
            lx = jnp.where(sub < 4, above[pl.ds(at + 152, 8), :], below[pl.ds(at + 152, 8), :])
            r2 = roll(jnp.where((sub >= 4), above[pl.ds(at, 8), :], below[pl.ds(at, 8), :]), 4, 0)
            l2 = roll(jnp.where((sub >= 4), above[pl.ds(at + 152, 8), :], below[pl.ds(at + 152, 8), :]), 4, 0)
            for i in range(16):
                layer = g * 16 + i
                pick = lambda p, q: jnp.where(lane < 64, roll(p, -8 * i, 1), roll(q, 120 - 8 * i, 1))
                ext[layer, 0:8, 0:128] = ref[layer]
                ext[layer, 0:8, 128:256] = pick(r, l)
                ext[layer, 8:16, 128:256] = pick(rx, lx)
                ext[layer, 16:24, 128:256] = pick(r2, l2)
                block, j = a * 24 + g * 4 + i // 4, 6 * (i % 4)
                ext[layer, 8:12, 0:128] = high[block, j : j + 4, :]
                ext[layer, 12:16, 0:128] = low[block, j + 2 : j + 6, :]
                ext[layer, 16:18, 0:128] = high[block, j + 4 : j + 6, :]
                ext[layer, 18:22, 0:128] = jnp.zeros((4, 128), F32)
                ext[layer, 22:24, 0:128] = low[block, j : j + 2, :]
            return 0

        lax.fori_loop(0, layers // 16, group, 0)

    leak[0:8, :] = gathered[2:10, :]
    leak[0:2, :] += leak_low[6:8, :]
    leak[6:8, :] += leak_high[0:2, :]
    leak[8:12, :] = leak_high[2:6, :]
    leak[8:10, :] += gathered[10:12, :]
    leak[12:16, :] = leak_low[2:6, :]
    leak[14:16, :] += gathered[0:2, :]
    leak[16:18, :] = leak_high[6:8, :]
    leak[18:22, :] = jnp.zeros((4, 768), F32)
    leak[22:24, :] = leak_low[0:2, :]

    def get(ref, at, n, width=256):
        return [ref[at, 8 * t : 8 * t + 8, 0:width] for t in range(n)]

    def put(ref, at, values):
        for t, x in enumerate(values):
            ref[at, 8 * t : 8 * t + 8, 0 : x.shape[1]] = x

    def leak_of(term, n, width=256):
        return [leak[8 * t : 8 * t + 8, 256 * term : 256 * term + width] for t in range(n)]

    zeros = lambda n, width=256: [jnp.zeros((8, width), F32)] * n

    put(vv, 0, zeros(3))
    put(vv, layers, zeros(3))
    put(vv, layers + 1, zeros(3))
    put(ip, layers, zeros(3))
    put(uu, layers, zeros(3))
    put(hy, layers, zeros(3))
    put(cz, layers, zeros(3))

    def links(t, carry):
        v_below, p_part, cond_below = carry
        at = layers - 1 - t
        k = [jnp.where(m > 0, x, 1.0) for m, x in zip(masks, get(kk, at, 3))]
        rock = [jnp.sqrt(x) * m for m, x in zip(masks, k)]
        put(wx, at, [time_step * a * b for a, b in zip(rock, up(rock))])
        put(wy, at, [time_step * a * b for a, b in zip(rock, nxt(rock))])
        v = [2.0 * a * b / (a + b) for a, b in zip(k, cond_below)]
        v = [jnp.where(at == layers - 1, 0.0, x) for x in v]
        put(vv, at + 1, v)
        inverse = [1.0 / (p + x) for p, x in zip(p_part, v)]
        u = [x * y for x, y in zip(v, inverse)]
        put(ip, at + 1, inverse)
        put(uu, at + 1, u)
        return v, [1.0 + x * (1.0 - y) for x, y in zip(v, u)], k

    _, pivot, _ = lax.fori_loop(0, layers, links, (zeros(3), [jnp.ones((8, 256), F32)] * 3, [jnp.ones((8, 256), F32)] * 3))
    put(ip, 0, [1.0 / (p + x) for p, x in zip(pivot, leak_of(0, 3))])
    put(uu, 0, zeros(3))

    def salt_pivot(at, carry):
        q_part = carry
        v = get(vv, at + 1, 3)
        q = [p + spread_vertical * x for p, x in zip(q_part, v)]
        inverse = [1.0 / x for x in q]
        k = [spread_vertical * x * y for x, y in zip(v, inverse)]
        put(iq, at, inverse)
        put(kk, at, k)
        return [porosity + spread_vertical * x * (1.0 - y) for x, y in zip(v, k)]

    lax.fori_loop(0, layers, salt_pivot, [porosity + x for x in leak_of(0, 3)])

    for step in range(AQ_ITERS):
        n_in = 3 if step < 2 else 2
        n_out = 3 if step == 0 else (1 if step == AQ_ITERS - 1 else 2)
        width = 128 if step == AQ_ITERS - 1 else 256

        def cut(values, n_out=n_out, width=width):
            return [x[:, 0:width] for x in values[:n_out]]

        def climb(t, carry, step=step, n_in=n_in, n_out=n_out, width=width, cut=cut):
            c_below, part, y_below = carry
            at = layers - 1 - t
            c = get(cz, at, n_in)
            if step > 0:
                c = [z + k * x for z, k, x in zip(c, get(kk, at, n_in), c_below)]
                put(cz, at, c)
            v = get(vv, at + 1, n_out, width)
            v_below = get(vv, at + 2, n_out, width)
            lift = [(0.5 * density_slope) * x * (a + b) for x, a, b in zip(v, cut(c), cut(c_below))]
            y = [
                (p + l + x * y) * i
                for p, l, x, y, i in zip(part, lift, v_below, y_below, get(ip, at + 1, n_out, width))
            ]
            h = get(hy, at, n_in)
            put(hy, at + 1, y)
            flow, side = sides_of(h, c, get(wx, at, n_in), get(wy, at, n_in))
            put(ss, at, [porosity * a + b for a, b in zip(cut(c), cut(side))])
            part = [a + b - l for a, b, l in zip(cut(h), cut(flow), lift)]
            return c, part, y

        _, part, y = lax.fori_loop(
            0, layers, climb, (zeros(n_in), zeros(n_out, width), zeros(n_out, width))
        )
        h = [
            (p + l + x * y) * i
            for p, l, x, y, i in zip(
                part, leak_of(1, n_out, width), get(vv, 1, n_out, width), y, get(ip, 0, n_out, width)
            )
        ]
        last = step == AQ_ITERS - 1
        put(head_out if last else hy, 0, h)
        put(ss, 0, [a + b for a, b in zip(get(ss, 0, n_out, width), leak_of(2, n_out, width))])

        def descend(at, carry, n_out=n_out, width=width, last=last):
            h_above, c_above, carried_above, z_above = carry
            h = [y + u * x for y, u, x in zip(get(hy, at, n_out, width), get(uu, at, n_out, width), h_above)]
            put(head_out if last else hy, at, h)
            c = get(cz, at, n_out, width)
            v = get(vv, at, n_out, width)
            rising = [
                x * (time_step * (a - b) - (0.5 * density_slope * time_step) * (p + q))
                for x, a, b, p, q in zip(v, h, h_above, c, c_above)
            ]
            carried = [r * jnp.where(r > 0, p, q) for r, p, q in zip(rising, c, c_above)]
            z = [
                (s + a - b + y) * i
                for s, a, b, y, i in zip(
                    get(ss, at - 1, n_out, width), carried, carried_above, z_above, get(iq, at - 1, n_out, width)
                )
            ]
            put(cz, at - 1, z)
            return h, c, carried, [spread_vertical * x * y for x, y in zip(v, z)]

        _, _, carried, z = lax.fori_loop(
            1, layers, descend, (h, get(cz, 0, n_out, width), zeros(n_out, width), zeros(n_out, width))
        )
        put(
            cz,
            layers - 1,
            [
                (s - b + y) * i
                for s, b, y, i in zip(
                    get(ss, layers - 1, n_out, width), carried, z, get(iq, layers - 1, n_out, width)
                )
            ],
        )

    def finish(t, c_below):
        at = layers - 1 - t
        c = cz[at, 0:8, 0:128] + kk[at, 0:8, 0:128] * c_below
        salt_out[at] = c
        return c

    lax.fori_loop(0, layers, finish, jnp.zeros((8, 128), F32))


def local(surf_depth, surf_bed, surf_conv, wet_mask, surf_salt, seabed_leak, seabed_shift, active_count, aq_head, aq_salt, aq_cond):
    shifts = seabed_shift.reshape(-1, 2)
    counts = active_count.reshape(1, -1)
    layers = aq_head.shape[0]
    aq = (aq_head, aq_salt, aq_cond)
    rim = (152, 128)
    in_low, in_high, rows_low, rows_high = call(
        pack_inland, [rim, rim, (8, 128), (8, 128)], (*aq, surf_depth, surf_bed, surf_conv, wet_mask), "pack_inland"
    )
    right = shift(in_low, "gy", -1)
    left = shift(in_high, "gy", 1)
    dense = (3 * layers // 4, 24, 128)
    coast_low, coast_high = call(pack_coast, [dense, dense], aq, "pack_coast")
    high = shift(coast_low, "gx", -1)
    low = shift(coast_high, "gx", 1)
    joined = (312, 128)
    join_low, join_high = call(join_rims, [joined, joined], (right, left, rows_low, rows_high), "join_rims")
    above = shift(join_low, "gx", -1)
    below = shift(join_high, "gx", 1)
    depth, to_low, to_high, to_low2, to_high2, own = call(
        surface,
        [(128, 128), (32, 384), (32, 384), (16, 384), (16, 384), (16, 768)],
        (surf_depth, surf_bed, surf_conv, wet_mask, surf_salt, seabed_leak, shifts, counts, right, left, above, below),
        "surface",
        scratch=[pltpu.VMEM((136, 256), F32)] * 2,
        keep=(0,),
    )
    leak_right = shift(to_low, "gy", -1)
    leak_left = shift(to_high, "gy", 1)
    leak_right2 = shift(to_low2, "gy", -2)
    leak_left2 = shift(to_high2, "gy", 2)
    gathered, sum_low, sum_high = call(
        sum_inland, [(16, 768), (8, 768), (8, 768)], (own, leak_right, leak_left, leak_right2, leak_left2), "sum_inland"
    )
    leak_high = shift(sum_low, "gx", -1)
    leak_low = shift(sum_high, "gx", 1)
    whole = pltpu.VMEM((layers + 2, 24, 256), F32)
    head, salt = call(
        aquifer,
        [aq_head.shape, aq_head.shape],
        (*aq, right, left, above, below, high, low, gathered, leak_high, leak_low),
        "aquifer",
        scratch=[whole] * 10 + [pltpu.VMEM((24, 768), F32)],
        keep=(0, 1),
    )
    return depth, head, salt


def solution(mesh):
    in_specs = (
        P("gx", "gy"),
        P("gx", "gy"),
        P("gx", "gy"),
        P("gx", "gy"),
        P("gx", "gy"),
        P("gx", "gy"),
        P("gx", "gy", None, None),
        P("gx", "gy", None),
        P(None, "gx", "gy"),
        P(None, "gx", "gy"),
        P(None, "gx", "gy"),
    )
    out_specs = (P("gx", "gy"), P(None, "gx", "gy"), P(None, "gx", "gy"))
    return jax.shard_map(local, mesh=mesh, in_specs=in_specs, out_specs=out_specs, check_vma=False)
```

```python
import functools

import jax
import jax.numpy as jnp
from jax import lax
from jax.experimental import pallas as pl
from jax.experimental.pallas import tpu as pltpu
from jax.sharding import PartitionSpec as P

SURF_STEPS = 4
AQ_ITERS = 6
HALO = 6

surface_rate = 0.24
time_step = 0.05
density_slope = 0.025
porosity = 0.35
spread_side = 0.1
spread_vertical = 0.1

F32 = jnp.float32
VMEM_LIMIT = 40 * 2**20
UNROLL = 8


def shift(block, axis, step):
    count = lax.axis_size(axis)
    return lax.ppermute(block, axis, [(i, (i + step) % count) for i in range(count)])


def call(body, outs, args, name, scratch=(), keep=None):
    shapes = [
        jax.ShapeDtypeStruct(shape, F32) if keep is not None and i in keep else pltpu.VMEM(shape, F32)
        for i, shape in enumerate(outs)
    ]
    return pl.pallas_call(
        body,
        out_shape=shapes,
        in_specs=[pl.BlockSpec(memory_space=pltpu.VMEM)] * len(args),
        out_specs=[pl.BlockSpec(memory_space=pltpu.VMEM)] * len(outs),
        scratch_shapes=list(scratch),
        compiler_params=pltpu.CompilerParams(vmem_limit_bytes=VMEM_LIMIT),
        name=name,
    )(*args)


def lanes(shape):
    return lax.broadcasted_iota(jnp.int32, shape, len(shape) - 1)


def rows_of(shape):
    return lax.broadcasted_iota(jnp.int32, shape, len(shape) - 2)


def roll(x, by, axis):
    by = by % x.shape[axis]
    return x if by == 0 else pltpu.roll(x, by, axis)


def pack_lanes(tiles, lane):
    low = tiles[0]
    high = roll(tiles[0], 8, 1)
    for i in range(1, len(tiles)):
        here = lane >= 8 * i
        low = jnp.where(here, roll(tiles[i], 8 * i, 1), low)
        high = jnp.where(here, roll(tiles[i], 8 * i + 8, 1), high)
    return low, high


def pack_inland(head, salt, cond, depth, bed, conv, wet, to_low, to_high, rows_low, rows_high):
    lane = lanes((8, 128))
    sub = rows_of((8, 128))
    level_rows, conduct_rows, tiles = [], [], []
    for t in range(16):
        here = slice(8 * t, 8 * t + 8)
        level = bed[here, :] + depth[here, :]
        conduct = wet[here, :].astype(F32) * jnp.sqrt(conv[here, :])
        level_rows.append(level)
        conduct_rows.append(conduct)
        tiles.append((jnp.where(lane < 4, level, roll(conduct, 4, 1)), jnp.where(lane < 4, roll(level, 4, 1), roll(conduct, 8, 1))))
    low, high = tiles[0]
    for t in range(1, 16):
        here = lane >= 8 * t
        low = jnp.where(here, roll(tiles[t][0], 8 * t, 1), low)
        high = jnp.where(here, roll(tiles[t][1], 8 * t, 1), high)
    to_low[144:152, :] = low
    to_high[144:152, :] = high
    rows_low[...] = jnp.where(sub < 4, level_rows[0], roll(conduct_rows[0], 4, 0))
    rows_high[...] = jnp.where(sub >= 4, level_rows[15], roll(conduct_rows[15], 4, 0))
    for a, ref in enumerate((head, salt, cond)):
        def group(g, _, a=a, ref=ref):
            first = [ref[g * 8 + i] for i in range(8)]
            low, high = pack_lanes(first + [ref[ref.shape[0] - 1 - g * 8 - i] for i in range(8)], lane)
            at = pl.ds(pl.multiple_of((a * 6 + g) * 8, 8), 8)
            to_low[at, :] = low
            to_high[at, :] = high
            return 0

        lax.fori_loop(0, 6, group, 0)


def join_rims(right, left, rows_low, rows_high, to_low, to_high):
    for out, rows in ((to_low, rows_low), (to_high, rows_high)):
        out[0:8, :] = right[144:152, :]
        out[8:16, :] = left[144:152, :]
        out[16:24, :] = rows[...]


def inside(shape, row_low, row_high, col_low, col_high):
    gx, gy = lax.axis_index("gx"), lax.axis_index("gy")
    last_x, last_y = lax.axis_size("gx") - 1, lax.axis_size("gy") - 1
    one = jnp.ones(shape, F32)
    zero = jnp.zeros(shape, F32)
    has = lambda there: jnp.where(there, 1.0, 0.0).astype(F32)
    row = jnp.where(row_high, one * has(gx < last_x), jnp.where(row_low, one * has(gx > 0), one))
    lane = lanes(shape)
    col = jnp.where(
        lane < 128,
        one,
        jnp.where(
            lane < 128 + col_high,
            one * has(gy < last_y),
            jnp.where(lane >= 256 - col_low, one * has(gy > 0), zero),
        ),
    )
    return row * col


def dot(a, b, dims):
    return lax.dot_general(a, b, (dims, ((), ())), precision=lax.Precision.HIGHEST, preferred_element_type=F32)


def surface(depth, bed, conv, wet, salt, leak, shifts, counts, right, left, above, below, depth_out, to_low, to_high, to_low2, to_high2, own, level_ref, conduct_ref):
    lane = lanes((8, 128))
    sub = rows_of((8, 128))
    ring = lanes((8, 256))
    sub_ring = rows_of((8, 256))
    column_in = inside((8, 256), sub_ring < 0, sub_ring < 0, 4, 4)
    corner_in = inside((8, 256), sub_ring >= 4, sub_ring < 4, 4, 4)

    def sides(r, l, t):
        level = jnp.where(lane < 4, roll(r, -8 * t, 1), roll(l, 124 - 8 * t, 1))
        conduct = jnp.where(lane < 4, roll(r, -8 * t - 4, 1), roll(l, 120 - 8 * t, 1))
        return level, conduct

    r, l = right[144:152, :], left[144:152, :]
    for t in range(16):
        here = slice(8 * t, 8 * t + 8)
        level, conduct = sides(r, l, t)
        level_ref[here, 0:128] = bed[here, :] + depth[here, :]
        level_ref[here, 128:256] = level
        conduct_ref[here, 0:128] = wet[here, :].astype(F32) * jnp.sqrt(conv[here, :])
        conduct_ref[here, 128:256] = conduct * column_in[:, 128:]
    high_rows, low_rows = above[16:24, :], below[16:24, :]
    high_sides = sides(above[0:8, :], above[8:16, :], 0)
    low_sides = sides(below[0:8, :], below[8:16, :], 15)
    level_ref[128:136, 0:128] = jnp.where(sub < 4, high_rows, low_rows)
    level_ref[128:136, 128:256] = jnp.where(sub < 4, high_sides[0], low_sides[0])
    conduct_ref[128:136, 0:128] = roll(jnp.where(sub >= 4, high_rows, low_rows), 4, 0) * corner_in[:, :128]
    conduct_ref[128:136, 128:256] = jnp.where(sub < 4, high_sides[1], low_sides[1]) * corner_in[:, 128:]

    level = level_ref[...]
    conduct = conduct_ref[...]
    link_x = surface_rate * conduct * roll(conduct, -1, 0)
    link_y = surface_rate * conduct * roll(conduct, -1, 1)
    final = depth[...]
    total = jnp.zeros((128, 128), F32)
    for _ in range(SURF_STEPS):
        flow_x = link_x * (roll(level, -1, 0) - level)
        flow_y = link_y * (roll(level, -1, 1) - level)
        moved = (flow_x - roll(flow_x, 1, 0)) + (flow_y - roll(flow_y, 1, 1))
        level = level + moved
        final = final + moved[0:128, 0:128]
        total = total + level[0:128, 0:128]
    depth_out[...] = final
    mean_level = total * (1.0 / SURF_STEPS)

    square = (128, 128)
    count = jnp.transpose(jnp.broadcast_to(counts[...].astype(F32), square))
    active = jnp.where(lanes(square).astype(F32) < count, 1.0, 0.0)
    cells = wet[...].astype(F32) * active * leak[...]
    gx, gy = lax.axis_index("gx"), lax.axis_index("gy")
    last_row, last_tile = 8 * lax.axis_size("gx") - 1, lax.axis_size("gy") - 1
    block = rows_of((128, 1))
    global_row = gx * 128 + block + shifts[:, 0:1]
    row = jnp.clip(jnp.right_shift(global_row, 4), 0, last_row) - gx * 8 + 2
    tile = jnp.clip(gy + shifts[:, 1:2], 0, last_tile) - gy + 1
    target = tile * 16 + row
    choose = jnp.where(lanes((128, 128)) == target, 1.0, 0.0)
    choose = jnp.transpose(choose)[0:48]
    sums = [dot(choose, term, ((1,), (0,))) for term in (cells, cells * mean_level, cells * salt[...])]
    lane48 = lanes((16, 128))
    for i, total in enumerate(sums):
        at = slice(128 * i, 128 * i + 128)
        to_low[:, at] = total[0:32]
        to_high[:, at] = total[16:48]
        to_low2[:, at] = total[0:16]
        to_high2[:, at] = total[32:48]
        own[:, 256 * i : 256 * i + 128] = total[16:32]
        own[:, 256 * i + 128 : 256 * i + 256] = jnp.where(lane48 < 8, total[32:48], jnp.where(lane48 >= 120, total[0:16], 0.0))


def sum_inland(own, right, left, right2, left2, gathered, to_low, to_high):
    lane = lanes((16, 128))
    for i in range(3):
        at = slice(128 * i, 128 * i + 128)
        first = slice(256 * i, 256 * i + 128)
        second = slice(256 * i + 128, 256 * i + 256)
        here = own[:, first] + right[0:16, at] + left[16:32, at]
        beside = own[:, second] + jnp.where(
            lane < 8,
            right[16:32, at] + right2[:, at],
            jnp.where(lane >= 120, left[0:16, at] + left2[:, at], 0.0),
        )
        gathered[:, first] = here
        gathered[:, second] = beside
    to_low[...] = gathered[0:8, :]
    to_high[...] = gathered[4:12, :]


J = 3


def column(lane, j):
    return J * jnp.bitwise_and(lane, 63) + (j - 8)


def take(x, index):
    return jnp.take_along_axis(x, index, axis=1)


def interleave(head, salt, cond, *outs):
    lane = lanes((8, 128))
    index = [jnp.clip(column(lane, j), 0, 127) for j in range(J)]
    for ref, out in zip((head, salt, cond), outs):
        last = ref.shape[0] - 1

        def pair(t, _, ref=ref, out=out, last=last):
            for e in range(2):
                at = 2 * t + e
                x, y = ref[at], ref[last - at]
                for j in range(J):
                    out[at, 8 * j : 8 * j + 8, :] = jnp.where(lane < 64, take(x, index[j]), take(y, index[j]))
            return 0

        lax.fori_loop(0, (last + 1) // 4, pair, 0)


def pack_coast(head, salt, cond, right, left, after, rim, to_low, to_high):
    del after
    lane = lanes((8, 128))
    group = jnp.right_shift(lane, 3)
    half = jnp.bitwise_and(lane, 64)
    inner = jnp.bitwise_and(lane, 63)
    even = jnp.bitwise_and(group, 1) == 0
    for a, ref in enumerate((head, salt, cond)):
        def eight(q, _, a=a, ref=ref):
            at = pl.multiple_of((a * 6 + q) * 8, 8)
            r, l = right[pl.ds(at, 8), :], left[pl.ds(at, 8), :]
            rims = (jnp.where(even, r, roll(l, 8, 1)), jnp.where(even, roll(l, -8, 1), r))
            for h in range(2):
                for j in range(J):
                    y = column(lane, j)
                    tiles = []
                    for e in range(4 * h, 4 * h + 4):
                        source = 8 * e + half + jnp.where(y < 0, y + (16 if e % 2 == 0 else 0), y - 128)
                        source = jnp.clip(source, 0, 127)
                        x = ref[q * 8 + e, 8 * j : 8 * j + 8, :]
                        x = jnp.where((y < 0) | (y >= 128), take(rims[e % 2], source), x)
                        rim[a * 48 + q * 8 + e, 8 * j : 8 * j + 8, :] = x
                        tiles.append(x)
                    for p in range(3):
                        m = 6 * ((h * J + j) * 3 + p)
                        full = jnp.where(inner < 48, tiles[p], roll(tiles[3], 48 - 16 * p, 1))
                        to_low[a * 6 + q, m : m + 6, :] = full[0:6]
                        to_high[a * 6 + q, m : m + 6, :] = full[2:8]
            return 0

        lax.fori_loop(0, 6, eight, 0)


def up(t):
    s = rows_of((8, 128))
    out = [None] * len(t)
    for j in range(J):
        x = t[j::J]
        r = [roll(y, -1, 0) for y in x]
        if len(x) == 2:
            new = [jnp.where(s == 7, r[1], r[0]), jnp.where(s == 7, r[0], r[1])]
        else:
            new = [
                jnp.where(s == 7, r[1], r[0]),
                jnp.where(s == 7, r[0], jnp.where(s == 3, roll(x[2], 3, 0), r[1])),
                jnp.where(s == 7, roll(x[1], 3, 0), r[2]),
            ]
        out[j::J] = new
    return out


def down(t):
    s = rows_of((8, 128))
    out = [None] * len(t)
    for j in range(J):
        x = t[j::J]
        r = [roll(y, 1, 0) for y in x]
        if len(x) == 2:
            new = [jnp.where(s == 0, r[1], r[0]), jnp.where(s == 0, r[0], r[1])]
        else:
            new = [
                jnp.where(s == 0, r[1], r[0]),
                jnp.where(s == 0, r[0], jnp.where(s == 4, roll(x[2], 5, 0), r[1])),
                jnp.where(s == 0, roll(x[1], 5, 0), r[2]),
            ]
        out[j::J] = new
    return out


def nxt(t):
    return [y for i in range(0, len(t), J) for y in (t[i + 1], t[i + 2], roll(t[i], -1, 1))]


def prv(t):
    return [y for i in range(0, len(t), J) for y in (roll(t[i + 2], 1, 1), t[i], t[i + 1])]


def swap(t):
    return [roll(x, 64, 1) for x in t]


def sides_of(h, c, wx, wy):
    flow = salt = None
    for w, ahead, back in ((wx, up, down), (wy, nxt, prv)):
        hs, cs = ahead(h), ahead(c)
        f, g = [], []
        for i in range(len(h)):
            dh = hs[i] - h[i]
            moved = dh * jnp.where(dh > 0, cs[i], c[i]) + spread_side * (cs[i] - c[i])
            f.append(w[i] * dh)
            g.append(w[i] * moved)
        fb, gb = back(f), back(g)
        f = [a - b for a, b in zip(f, fb)]
        g = [a - b for a, b in zip(g, gb)]
        flow = f if flow is None else [a + b for a, b in zip(flow, f)]
        salt = g if salt is None else [a + b for a, b in zip(salt, g)]
    return flow, salt


def get(ref, at, n):
    return [ref[at, 8 * m : 8 * m + 8, :] for m in range(n)]


def put(ref, at, values):
    for m, x in enumerate(values):
        ref[at, 8 * m : 8 * m + 8, :] = x


def sweep(first, count, body, carry, unroll=None):
    unroll = unroll or UNROLL
    turns = count // unroll

    def turn(t, carry):
        for i in range(unroll):
            carry = body(first + t * unroll + i, carry)
        return carry

    carry = lax.fori_loop(0, turns, turn, carry)
    for i in range(turns * unroll, count):
        carry = body(first + i, carry)
    return carry


def zeros(n):
    return [jnp.zeros((8, 128), F32)] * n


def tilt():
    size = 0.5 * density_slope
    return jnp.where(lanes((8, 128)) < 64, size, -size).astype(F32)


def prepare(rim, high, low, part, side, salt, wx, wy, vv, head, cond, stage):
    steps = salt.shape[0]
    n = 3 * J
    lane = lanes((8, 128))
    sub = rows_of((8, 128))
    inner = jnp.bitwise_and(lane, 63)
    stage[...] = jnp.zeros(stage.shape, F32)
    for a, ext in enumerate((head, salt, cond)):
        def eight(q, _, a=a, ext=ext):
            block = a * 6 + q
            for m in range(18):
                stage[m, 0:4, :] = high[block, 6 * m : 6 * m + 4, :]
                stage[m, 4:8, :] = low[block, 6 * m + 2 : 6 * m + 6, :]
                stage[m, 8:10, :] = high[block, 6 * m + 4 : 6 * m + 6, :]
                stage[m, 14:16, :] = low[block, 6 * m : 6 * m + 2, :]
            for h in range(2):
                for e in range(4):
                    ext[q * 8 + 4 * h + e, 0:24, :] = rim[a * 48 + q * 8 + 4 * h + e, 0:24, :]
                for j in range(J):
                    m = (h * J + j) * 3
                    for i in range(2):
                        x = [stage[m + p, 8 * i : 8 * i + 8, :] for p in range(3)]
                        x.append(
                            jnp.where(
                                inner < 16,
                                roll(x[0], -48, 1),
                                jnp.where(inner < 32, roll(x[1], -32, 1), roll(x[2], -16, 1)),
                            )
                        )
                        at = 24 * (i + 1) + 8 * j
                        for e in range(4):
                            ext[q * 8 + 4 * h + e, at : at + 8, :] = x[e]
            return 0

        lax.fori_loop(0, steps // 8, eight, 0)

    gx, gy = lax.axis_index("gx"), lax.axis_index("gy")
    last_x, last_y = lax.axis_size("gx") - 1, lax.axis_size("gy") - 1
    has = lambda there: jnp.where(there, 1.0, 0.0).astype(F32)
    beside = jnp.where(sub < 4, has(gx < last_x), has(gx > 0))
    rows = [jnp.ones((8, 128), F32), beside, beside * jnp.where((sub < 2) | (sub >= 6), 1.0, 0.0)]
    masks = []
    for i in range(3):
        for j in range(J):
            y = column(lane, j)
            in_low = jnp.where(y >= -HALO, has(gy > 0), 0.0)
            in_high = jnp.where(y < 128 + HALO, has(gy < last_y), 0.0)
            masks.append(rows[i] * jnp.where(inner < 48, jnp.where(y < 0, in_low, jnp.where(y < 128, 1.0, in_high)), 0.0))
    weigh = tilt()

    def known(at):
        return [jnp.where(m > 0, x, 1.0) for m, x in zip(masks, get(cond, at, n))]

    def one(at, carry, inmost=False):
        k, c, lift_above = carry
        k_in = swap(k) if inmost else known(at + 1)
        c_in = swap(c) if inmost else get(salt, at + 1, n)
        rock = [jnp.sqrt(x) * m for m, x in zip(masks, k)]
        x = [time_step * a * b for a, b in zip(rock, up(rock))]
        y = [time_step * a * b for a, b in zip(rock, nxt(rock))]
        v = [2.0 * a * b / (a + b) for a, b in zip(k, k_in)]
        put(wx, at, x)
        put(wy, at, y)
        put(vv, at, v)
        h = get(head, at, n)
        lift = [(weigh * b) * (p + q) for b, p, q in zip(v, c, c_in)]
        flow, moved = sides_of(h, c, x, y)
        put(part, at, [a + b - p + q for a, b, p, q in zip(h, flow, lift, lift_above)])
        put(side, at, [porosity * a + b for a, b in zip(c, moved)])
        return k_in, c_in, lift

    carry = sweep(0, steps - 1, one, (known(0), get(salt, 0, n), zeros(n)), 4)
    one(steps - 1, carry, True)


def aquifer(part0, side0, salt0, wx, wy, vv, gathered, leak_high, leak_low, head_out, salt_out, hy, cz, ss, ip, uu, iq, kk, mid, leak):
    steps = salt0.shape[0]
    layers = 2 * steps
    lane = lanes((8, 128))
    inner = jnp.bitwise_and(lane, 63)
    weigh = tilt()

    leak[0:8, :] = gathered[2:10, :]
    leak[0:2, :] += leak_low[6:8, :]
    leak[6:8, :] += leak_high[0:2, :]
    leak[8:12, :] = leak_high[2:6, :]
    leak[8:10, :] += gathered[10:12, :]
    leak[12:16, :] = leak_low[2:6, :]
    leak[14:16, :] += gathered[0:2, :]
    leak[16:18, :] = leak_high[6:8, :]
    leak[18:22, :] = jnp.zeros((4, 768), F32)
    leak[22:24, :] = leak_low[0:2, :]

    def leak_of(term, n):
        out = []
        for m in range(n):
            i, j = m // J, m % J
            y = column(lane, j)
            here = leak[8 * i : 8 * i + 8, 256 * term : 256 * term + 128]
            beside = leak[8 * i : 8 * i + 8, 256 * term + 128 : 256 * term + 256]
            x = jnp.where((y >= 0) & (y < 128), take(here, jnp.clip(y, 0, 127)), take(beside, jnp.bitwise_and(y, 127)))
            out.append(jnp.where(lane < 48, x, 0.0))
        return out

    n = 3 * J
    total, level = leak_of(0, n), leak_of(1, n)

    def pivots(at, carry):
        p, q, flow = carry
        v = get(vv, at, n)
        inverse = [1.0 / (a + b) for a, b in zip(p, v)]
        u = [a * b for a, b in zip(v, inverse)]
        put(ip, at, inverse)
        put(uu, at, u)
        y = [(a + b) * i for a, b, i in zip(get(part0, at, n), flow, inverse)]
        put(hy, at, y)
        inverse = [1.0 / (a + spread_vertical * b) for a, b in zip(q, v)]
        k = [spread_vertical * a * b for a, b in zip(v, inverse)]
        put(iq, at, inverse)
        put(kk, at, k)
        return (
            [1.0 + a * (1.0 - b) for a, b in zip(v, u)],
            [porosity + spread_vertical * a * (1.0 - b) for a, b in zip(v, k)],
            [a * b for a, b in zip(v, y)],
        )

    sweep(0, steps, pivots, ([1.0 + x for x in total], [porosity + x for x in total], level))
    for place, ref in enumerate((uu, kk)):
        u = get(ref, steps - 1, n)
        put(mid, place, [1.0 / (1.0 - a * b) for a, b in zip(u, swap(u))])

    def outward(state, ratio, place, n):
        y, u = get(state, steps - 1, n), get(ratio, steps - 1, n)
        x = [(a + b * c) * d for a, b, c, d in zip(y, u, swap(y), get(mid, place, n))]
        put(state, steps - 1, x)

        def back(t, x):
            at = steps - 2 - t
            x = [a + b * c for a, b, c in zip(get(state, at, n), get(ratio, at, n), x)]
            put(state, at, x)
            return x

        sweep(0, steps - 1, back, x)

    in_order = [jnp.right_shift((lane + 8 - j) * 21846, 16) for j in range(J)]
    owner = lane + 8 - 3 * jnp.right_shift((lane + 8) * 21846, 16)

    def write(out, at, x):
        for end in range(2):
            y = [take(z, jnp.clip(index, 0, 63) + 64 * end) for z, index in zip(x, in_order)]
            layer = at if end == 0 else layers - 1 - at
            out[layer] = jnp.where(owner == 0, y[0], jnp.where(owner == 1, y[1], y[2]))

    for step in range(AQ_ITERS):
        last = step == AQ_ITERS - 1
        n_in = J * (3 if step < 2 else 2)
        n = J * (3 if step == 0 else 1 if last else 2)
        salt = salt0 if step == 0 else cz
        if step > 0:
            def inward(at, carry, n_in=n_in, n=n, inmost=False):
                c, lift_above, flow_above = carry
                c_in = swap(c) if inmost else get(cz, at + 1, n_in)
                v = get(vv, at, n)
                lift = [(weigh * b) * (p + q) for b, p, q in zip(v, c, c_in)]
                h = get(hy, at, n_in)
                flow, moved = sides_of(h, c, get(wx, at, n_in), get(wy, at, n_in))
                y = [
                    (a + b - p + q + r) * i
                    for a, b, p, q, r, i in zip(h, flow, lift, lift_above, flow_above, get(ip, at, n))
                ]
                put(hy, at, y)
                put(ss, at, [porosity * a + b for a, b in zip(c[:n], moved)])
                return c_in, lift, [a * b for a, b in zip(v, y)]

            carry = sweep(0, steps - 1, inward, (get(cz, 0, n_in), zeros(n), leak_of(1, n)))
            inward(steps - 1, carry, inmost=True)
        outward(hy, uu, 0, n)

        source = side0 if step == 0 else ss

        def salt_inward(at, carry, n=n, salt=salt, source=source, last=last, inmost=False):
            h, c, carried_above, z_above = carry
            h_in = swap(h) if inmost else get(hy, at + 1, n)
            c_in = swap(c) if inmost else get(salt, at + 1, n)
            v = get(vv, at, n)
            rising = [
                x * (time_step * (a - b) - (time_step * weigh) * (p + q))
                for x, a, b, p, q in zip(v, h_in, h, c_in, c)
            ]
            carried = [r * jnp.where(r > 0, p, q) for r, p, q in zip(rising, c_in, c)]
            z = [
                (s + a - b + y) * i
                for s, a, b, y, i in zip(get(source, at, n), carried, carried_above, z_above, get(iq, at, n))
            ]
            put(cz, at, z)
            if last:
                write(head_out, at, h)
            return h_in, c_in, carried, [spread_vertical * x * y for x, y in zip(v, z)]

        carry = sweep(0, steps - 1, salt_inward, (get(hy, 0, n), get(salt, 0, n), zeros(n), leak_of(2, n)))
        salt_inward(steps - 1, carry, inmost=True)
        outward(cz, kk, 1, n)

    sweep(0, steps, lambda at, _: write(salt_out, at, get(cz, at, J)) or 0, 0)


def whole(steps):
    return (steps, 24 * J, 128)


def run_prepare(rim, high, low):
    steps = rim.shape[0] // 3
    return call(
        prepare,
        [whole(steps)] * 6,
        (rim, high, low),
        "prepare",
        scratch=[pltpu.VMEM(whole(steps), F32)] * 2 + [pltpu.VMEM((18, 16, 128), F32)],
    )


def run_aquifer(*args):
    steps = args[0].shape[0]
    return call(
        aquifer,
        [(2 * steps, 8, 128)] * 2,
        args,
        "aquifer",
        scratch=[pltpu.VMEM(whole(steps), F32)] * 7 + [pltpu.VMEM((2, 24 * J, 128), F32), pltpu.VMEM((24, 768), F32)],
        keep=(0, 1),
    )


def local(surf_depth, surf_bed, surf_conv, wet_mask, surf_salt, seabed_leak, seabed_shift, active_count, aq_head, aq_salt, aq_cond):
    shifts = seabed_shift.reshape(-1, 2)
    counts = active_count.reshape(1, -1)
    steps = aq_head.shape[0] // 2
    aq = (aq_head, aq_salt, aq_cond)
    rim = (152, 128)
    in_low, in_high, rows_low, rows_high = call(
        pack_inland, [rim, rim, (8, 128), (8, 128)], (*aq, surf_depth, surf_bed, surf_conv, wet_mask), "pack_inland"
    )
    right = shift(in_low, "gy", -1)
    left = shift(in_high, "gy", 1)
    tiles = call(interleave, [(steps, 8 * J, 128)] * 3, aq, "interleave")
    join_low, join_high = call(join_rims, [(24, 128)] * 2, (right, left, rows_low, rows_high), "join_rims")
    above = shift(join_low, "gx", -1)
    below = shift(join_high, "gx", 1)
    rims, coast_low, coast_high = call(
        pack_coast,
        [(3 * steps, 8 * J, 128), (18, 112, 128), (18, 112, 128)],
        (*tiles, right, left, join_low),
        "pack_coast",
    )
    high = shift(coast_low, "gx", -1)
    low = shift(coast_high, "gx", 1)
    depth, to_low, to_high, to_low2, to_high2, own = call(
        surface,
        [(128, 128), (32, 384), (32, 384), (16, 384), (16, 384), (16, 768)],
        (surf_depth, surf_bed, surf_conv, wet_mask, surf_salt, seabed_leak, shifts, counts, right, left, above, below),
        "surface",
        scratch=[pltpu.VMEM((136, 256), F32)] * 2,
        keep=(0,),
    )
    leak_right = shift(to_low, "gy", -1)
    leak_left = shift(to_high, "gy", 1)
    leak_right2 = shift(to_low2, "gy", -2)
    leak_left2 = shift(to_high2, "gy", 2)
    ready = run_prepare(rims, high, low)
    gathered, sum_low, sum_high = call(
        sum_inland, [(16, 768), (8, 768), (8, 768)], (own, leak_right, leak_left, leak_right2, leak_left2), "sum_inland"
    )
    leak_high = shift(sum_low, "gx", -1)
    leak_low = shift(sum_high, "gx", 1)
    head, salt = run_aquifer(*ready, gathered, leak_high, leak_low)
    return depth, head, salt


def solution(mesh):
    in_specs = (
        P("gx", "gy"),
        P("gx", "gy"),
        P("gx", "gy"),
        P("gx", "gy"),
        P("gx", "gy"),
        P("gx", "gy"),
        P("gx", "gy", None, None),
        P("gx", "gy", None),
        P(None, "gx", "gy"),
        P(None, "gx", "gy"),
        P(None, "gx", "gy"),
    )
    out_specs = (P("gx", "gy"), P(None, "gx", "gy"), P(None, "gx", "gy"))
    return jax.shard_map(local, mesh=mesh, in_specs=in_specs, out_specs=out_specs, check_vma=False)
```

```python
import functools

import jax
import jax.numpy as jnp
from jax import lax
from jax.experimental import pallas as pl
from jax.experimental.pallas import tpu as pltpu
from jax.sharding import PartitionSpec as P

SURF_STEPS = 4
AQ_ITERS = 6
HALO = 6

surface_rate = 0.24
time_step = 0.05
density_slope = 0.025
porosity = 0.35
spread_side = 0.1
spread_vertical = 0.1

F32 = jnp.float32
VMEM_LIMIT = 20 * 2**20
UNROLL = 8


def shift(block, axis, step):
    count = lax.axis_size(axis)
    return lax.ppermute(block, axis, [(i, (i + step) % count) for i in range(count)])


def call(body, outs, args, name, scratch=(), keep=(), raw=(), micros=1.0):
    outs = [x if isinstance(x, jax.core.ShapedArray) else jax.ShapeDtypeStruct(x, F32) for x in outs]
    shapes = [x if i in keep else pltpu.VMEM(x.shape, x.dtype) for i, x in enumerate(outs)]
    args = [pltpu.with_memory_space_constraint(x, pltpu.HBM) if i in raw else x for i, x in enumerate(args)]
    spec = lambda i: pl.BlockSpec(memory_space=pltpu.HBM if i in raw else pltpu.VMEM)
    return pl.pallas_call(
        body,
        out_shape=shapes,
        in_specs=[spec(i) for i in range(len(args))],
        out_specs=[pl.BlockSpec(memory_space=pltpu.VMEM)] * len(outs),
        scratch_shapes=list(scratch),
        compiler_params=pltpu.CompilerParams(vmem_limit_bytes=VMEM_LIMIT),
        cost_estimate=pl.CostEstimate(flops=0, bytes_accessed=int(micros * 3.5e6), transcendentals=0),
        name=name,
    )(*args)


def behind(arrays, *first):
    def body(*refs):
        del refs

    count = len(arrays)
    return pl.pallas_call(
        body,
        out_shape=[pltpu.VMEM(x.shape, x.dtype) for x in arrays],
        in_specs=[pl.BlockSpec(memory_space=pltpu.VMEM)] * (count + len(first)),
        out_specs=[pl.BlockSpec(memory_space=pltpu.VMEM)] * count,
        input_output_aliases={i: i for i in range(count)},
        compiler_params=pltpu.CompilerParams(vmem_limit_bytes=VMEM_LIMIT),
        name="behind",
    )(*arrays, *first)


def lanes(shape):
    return lax.broadcasted_iota(jnp.int32, shape, len(shape) - 1)


def rows_of(shape):
    return lax.broadcasted_iota(jnp.int32, shape, len(shape) - 2)


def roll(x, by, axis):
    by = by % x.shape[axis]
    return x if by == 0 else pltpu.roll(x, by, axis)


def pack_inland(*refs):
    args, (to_low, to_high, rows_low, rows_high), here, sems = refs[:11], refs[11:15], refs[15:26], refs[26]
    copies = [pltpu.make_async_copy(x, y, sems.at[i]) for i, (x, y) in enumerate(zip(args, here))]
    surf_copies, late_copies, aq_copies = copies[:4], copies[4:8], copies[8:]
    for copy in (*surf_copies, *aq_copies, *late_copies):
        copy.start()
    for copy in surf_copies:
        copy.wait()
    depth, bed, conv, wet = here[:4]
    lane = lanes((8, 128))
    sub = rows_of((8, 128))
    level_rows, conduct_rows, tiles = [], [], []
    for t in range(16):
        at = slice(8 * t, 8 * t + 8)
        level = bed[at, :] + depth[at, :]
        conduct = wet[at, :].astype(F32) * jnp.sqrt(conv[at, :])
        level_rows.append(level)
        conduct_rows.append(conduct)
        tiles.append((jnp.where(lane < 4, level, roll(conduct, 4, 1)), jnp.where(lane < 4, roll(level, 4, 1), roll(conduct, 8, 1))))
    low, high = tiles[0]
    for t in range(1, 16):
        at = lane >= 8 * t
        low = jnp.where(at, roll(tiles[t][0], 8 * t, 1), low)
        high = jnp.where(at, roll(tiles[t][1], 8 * t, 1), high)
    to_low[144:152, :] = low
    to_high[144:152, :] = high
    rows_low[...] = jnp.where(sub < 4, level_rows[0], roll(conduct_rows[0], 4, 0))
    rows_high[...] = jnp.where(sub >= 4, level_rows[15], roll(conduct_rows[15], 4, 0))
    first = jnp.bitwise_and(lane, 8) == 0
    for a in range(3):
        aq_copies[a].wait()
        ref = here[8 + a]
        last = ref.shape[0] - 1
        for q in range(6):
            ends = []
            for h in range(2):
                t = 8 * q + 4 * h
                layers = [t + e for e in range(4)] + [last - t - e for e in range(4)]
                x = roll(ref[layers[0]], 8, 1)
                for k in range(1, 8):
                    x = jnp.where(lane >= 16 * k, roll(ref[layers[k]], 16 * k + 8, 1), x)
                ends.append(x)
            at = slice((a * 6 + q) * 8, (a * 6 + q) * 8 + 8)
            to_low[at, :] = jnp.where(first, roll(ends[1], -8, 1), ends[0])
            to_high[at, :] = jnp.where(first, ends[0], roll(ends[1], 8, 1))
    for copy in late_copies:
        copy.wait()


def join_rims(right, left, rows_low, rows_high, after, to_low, to_high):
    del after
    for out, rows in ((to_low, rows_low), (to_high, rows_high)):
        out[0:8, :] = right[144:152, :]
        out[8:16, :] = left[144:152, :]
        out[16:24, :] = rows[...]


def inside(shape, row_low, row_high, col_low, col_high):
    gx, gy = lax.axis_index("gx"), lax.axis_index("gy")
    last_x, last_y = lax.axis_size("gx") - 1, lax.axis_size("gy") - 1
    one = jnp.ones(shape, F32)
    zero = jnp.zeros(shape, F32)
    has = lambda there: jnp.where(there, 1.0, 0.0).astype(F32)
    row = jnp.where(row_high, one * has(gx < last_x), jnp.where(row_low, one * has(gx > 0), one))
    lane = lanes(shape)
    col = jnp.where(
        lane < 128,
        one,
        jnp.where(
            lane < 128 + col_high,
            one * has(gy < last_y),
            jnp.where(lane >= 256 - col_low, one * has(gy > 0), zero),
        ),
    )
    return row * col


def dot(a, b, dims):
    return lax.dot_general(a, b, (dims, ((), ())), precision=lax.Precision.HIGHEST, preferred_element_type=F32)


def surface(depth, bed, conv, wet, salt, leak, shifts, counts, right, left, above, below, depth_out, to_low, to_high, to_low2, to_high2, own, level_ref, conduct_ref):
    lane = lanes((8, 128))
    sub = rows_of((8, 128))
    ring = lanes((8, 256))
    sub_ring = rows_of((8, 256))
    column_in = inside((8, 256), sub_ring < 0, sub_ring < 0, 4, 4)
    corner_in = inside((8, 256), sub_ring >= 4, sub_ring < 4, 4, 4)

    def sides(r, l, t):
        level = jnp.where(lane < 4, roll(r, -8 * t, 1), roll(l, 124 - 8 * t, 1))
        conduct = jnp.where(lane < 4, roll(r, -8 * t - 4, 1), roll(l, 120 - 8 * t, 1))
        return level, conduct

    r, l = right[144:152, :], left[144:152, :]
    for t in range(16):
        here = slice(8 * t, 8 * t + 8)
        level, conduct = sides(r, l, t)
        level_ref[here, 0:128] = bed[here, :] + depth[here, :]
        level_ref[here, 128:256] = level
        conduct_ref[here, 0:128] = wet[here, :].astype(F32) * jnp.sqrt(conv[here, :])
        conduct_ref[here, 128:256] = conduct * column_in[:, 128:]
    high_rows, low_rows = above[16:24, :], below[16:24, :]
    high_sides = sides(above[0:8, :], above[8:16, :], 0)
    low_sides = sides(below[0:8, :], below[8:16, :], 15)
    level_ref[128:136, 0:128] = jnp.where(sub < 4, high_rows, low_rows)
    level_ref[128:136, 128:256] = jnp.where(sub < 4, high_sides[0], low_sides[0])
    conduct_ref[128:136, 0:128] = roll(jnp.where(sub >= 4, high_rows, low_rows), 4, 0) * corner_in[:, :128]
    conduct_ref[128:136, 128:256] = jnp.where(sub < 4, high_sides[1], low_sides[1]) * corner_in[:, 128:]

    level = level_ref[...]
    conduct = conduct_ref[...]
    link_x = surface_rate * conduct * roll(conduct, -1, 0)
    link_y = surface_rate * conduct * roll(conduct, -1, 1)
    final = depth[...]
    total = jnp.zeros((128, 128), F32)
    for _ in range(SURF_STEPS):
        flow_x = link_x * (roll(level, -1, 0) - level)
        flow_y = link_y * (roll(level, -1, 1) - level)
        moved = (flow_x - roll(flow_x, 1, 0)) + (flow_y - roll(flow_y, 1, 1))
        level = level + moved
        final = final + moved[0:128, 0:128]
        total = total + level[0:128, 0:128]
    depth_out[...] = final
    mean_level = total * (1.0 / SURF_STEPS)

    square = (128, 128)
    count = jnp.transpose(jnp.broadcast_to(counts[...].astype(F32), square))
    active = jnp.where(lanes(square).astype(F32) < count, 1.0, 0.0)
    cells = wet[...].astype(F32) * active * leak[...]
    gx, gy = lax.axis_index("gx"), lax.axis_index("gy")
    last_row, last_tile = 8 * lax.axis_size("gx") - 1, lax.axis_size("gy") - 1
    block = lanes((1, 128))
    global_row = gx * 128 + block + shifts[0:1, :]
    row = jnp.clip(jnp.right_shift(global_row, 4), 0, last_row) - gx * 8 + 2
    tile = jnp.clip(gy + shifts[1:2, :], 0, last_tile) - gy + 1
    target = tile * 16 + row
    choose = jnp.where(rows_of((48, 128)) == target, 1.0, 0.0)
    sums = [dot(choose, term, ((1,), (0,))) for term in (cells, cells * mean_level, cells * salt[...])]
    lane48 = lanes((16, 128))
    for i, total in enumerate(sums):
        at = slice(128 * i, 128 * i + 128)
        to_low[:, at] = total[0:32]
        to_high[:, at] = total[16:48]
        to_low2[:, at] = total[0:16]
        to_high2[:, at] = total[32:48]
        own[:, 256 * i : 256 * i + 128] = total[16:32]
        own[:, 256 * i + 128 : 256 * i + 256] = jnp.where(lane48 < 8, total[32:48], jnp.where(lane48 >= 120, total[0:16], 0.0))


def sum_inland(own, right, left, right2, left2, gathered, to_low, to_high):
    lane = lanes((16, 128))
    for i in range(3):
        at = slice(128 * i, 128 * i + 128)
        first = slice(256 * i, 256 * i + 128)
        second = slice(256 * i + 128, 256 * i + 256)
        here = own[:, first] + right[0:16, at] + left[16:32, at]
        beside = own[:, second] + jnp.where(
            lane < 8,
            right[16:32, at] + right2[:, at],
            jnp.where(lane >= 120, left[0:16, at] + left2[:, at], 0.0),
        )
        gathered[:, first] = here
        gathered[:, second] = beside
    to_low[...] = gathered[0:8, :]
    to_high[...] = gathered[4:12, :]


J = 3


def column(lane, j):
    return J * jnp.bitwise_and(lane, 63) + (j - 8)


def take(x, index):
    return jnp.take_along_axis(x, index, axis=1)


def interleave(head, salt, cond, *outs):
    lane = lanes((8, 128))
    inner = jnp.bitwise_and(lane, 63)
    index = [jnp.clip(column(lane, j), 0, 127) for j in range(J)]
    for ref, out in zip((head, salt, cond), outs):
        last = ref.shape[0] - 1

        def eight(q, _, ref=ref, out=out, last=last):
            for h in range(2):
                for j in range(J):
                    x = []
                    for e in range(4):
                        at = q * 8 + 4 * h + e
                        x.append(jnp.where(lane < 64, take(ref[at], index[j]), take(ref[last - at], index[j])))
                    m = (h * J + j) * 3
                    for p in range(3):
                        out[q, m + p] = jnp.where(inner < 48, x[p], roll(x[3], 48 - 16 * p, 1))
            return 0

        lax.fori_loop(0, (last + 1) // 16, eight, 0)


def pack_coast(head, salt, cond, right, left, full, first_low, first_high, then_low, then_high):
    lane = lanes((8, 128))
    half = jnp.bitwise_and(lane, 64)
    inner = jnp.bitwise_and(lane, 63)
    odd = jnp.bitwise_and(lane, 8) != 0
    picks = []
    for h in range(2):
        for j in range(J):
            for p in range(3):
                mine = inner < 48
                y = J * jnp.where(mine, inner, inner - 48 + 16 * p) + (j - 8)
                e = jnp.where(mine, p, 3)
                right_at, left_at = (8, 0) if h == 0 else (0, 8)
                source = 16 * e + half + jnp.where(y < 0, left_at + 8 + y, right_at + y - 128)
                picks.append(((y < 0) | (y >= 128), jnp.clip(source, 0, 127)))
    ways = ((first_low, first_high, 6), (then_low, then_high, 0), (first_low, first_high, 0))
    for a, (ref, (to_low, to_high, start)) in enumerate(zip((head, salt, cond), ways)):
        def eight(q, _, a=a, ref=ref, to_low=to_low, to_high=to_high, start=start):
            at = pl.multiple_of((a * 6 + q) * 8, 8)
            r, l = right[pl.ds(at, 8), :], left[pl.ds(at, 8), :]
            rims = (jnp.where(odd, r, l), jnp.where(odd, l, r))
            for m in range(18):
                there, source = picks[m]
                x = jnp.where(there, take(rims[m // 9], source), ref[q, m])
                full[a * 6 + q, m] = x
                to_low[start + q, 6 * m : 6 * m + 6, :] = x[0:6]
                to_high[start + q, 6 * m : 6 * m + 6, :] = x[2:8]
            return 0

        lax.fori_loop(0, 6, eight, 0)


def fourth(x, inner):
    return jnp.where(inner < 16, roll(x[0], -48, 1), jnp.where(inner < 32, roll(x[1], -32, 1), roll(x[2], -16, 1)))


def open_tile(full, rim):
    inner = jnp.bitwise_and(lanes((8, 128)), 63)

    def eight(b, _):
        for h in range(2):
            for j in range(J):
                m = (h * J + j) * 3
                x = [full[b, m + p] for p in range(3)]
                x.append(fourth(x, inner))
                for e in range(4):
                    rim[b * 8 + 4 * h + e, 8 * j : 8 * j + 8, :] = x[e]
        return 0

    lax.fori_loop(0, 18, eight, 0)


def up(t):
    s = rows_of((8, 128))
    out = [None] * len(t)
    for j in range(J):
        x = t[j::J]
        r = [roll(y, -1, 0) for y in x]
        if len(x) == 2:
            new = [jnp.where(s == 7, r[1], r[0]), jnp.where(s == 7, r[0], r[1])]
        else:
            new = [
                jnp.where(s == 7, r[1], r[0]),
                jnp.where(s == 7, r[0], jnp.where(s == 3, roll(x[2], 3, 0), r[1])),
                jnp.where(s == 7, roll(x[1], 3, 0), r[2]),
            ]
        out[j::J] = new
    return out


def down(t):
    s = rows_of((8, 128))
    out = [None] * len(t)
    for j in range(J):
        x = t[j::J]
        r = [roll(y, 1, 0) for y in x]
        if len(x) == 2:
            new = [jnp.where(s == 0, r[1], r[0]), jnp.where(s == 0, r[0], r[1])]
        else:
            new = [
                jnp.where(s == 0, r[1], r[0]),
                jnp.where(s == 0, r[0], jnp.where(s == 4, roll(x[2], 5, 0), r[1])),
                jnp.where(s == 0, roll(x[1], 5, 0), r[2]),
            ]
        out[j::J] = new
    return out


def nxt(t):
    return [y for i in range(0, len(t), J) for y in (t[i + 1], t[i + 2], roll(t[i], -1, 1))]


def prv(t):
    return [y for i in range(0, len(t), J) for y in (roll(t[i + 2], 1, 1), t[i], t[i + 1])]


def swap(t):
    return [roll(x, 64, 1) for x in t]


def sides_of(h, c, wx, wy):
    flow = salt = None
    for w, ahead, back in ((wx, up, down), (wy, nxt, prv)):
        hs, cs = ahead(h), ahead(c)
        f, g = [], []
        for i in range(len(h)):
            dh = hs[i] - h[i]
            moved = dh * jnp.where(dh > 0, cs[i], c[i]) + spread_side * (cs[i] - c[i])
            f.append(w[i] * dh)
            g.append(w[i] * moved)
        fb, gb = back(f), back(g)
        f = [a - b for a, b in zip(f, fb)]
        g = [a - b for a, b in zip(g, gb)]
        flow = f if flow is None else [a + b for a, b in zip(flow, f)]
        salt = g if salt is None else [a + b for a, b in zip(salt, g)]
    return flow, salt


def get(ref, at, n):
    return [ref[at, 8 * m : 8 * m + 8, :] for m in range(n)]


def put(ref, at, values):
    for m, x in enumerate(values):
        ref[at, 8 * m : 8 * m + 8, :] = x


def sweep(first, count, body, carry, unroll=None):
    unroll = unroll or UNROLL
    turns = count // unroll

    def turn(t, carry):
        for i in range(unroll):
            carry = body(first + t * unroll + i, carry)
        return carry

    carry = lax.fori_loop(0, turns, turn, carry)
    for i in range(turns * unroll, count):
        carry = body(first + i, carry)
    return carry


def zeros(n):
    return [jnp.zeros((8, 128), F32)] * n


def tilt():
    size = 0.5 * density_slope
    return jnp.where(lanes((8, 128)) < 64, size, -size).astype(F32)


def unfold(a, rim, high, low, start, ext, stage):
    inner = jnp.bitwise_and(lanes((8, 128)), 63)

    def eight(q, _):
        block = start + q
        for m in range(18):
            stage[m, 0:4, :] = high[block, 6 * m : 6 * m + 4, :]
            stage[m, 4:8, :] = low[block, 6 * m + 2 : 6 * m + 6, :]
            stage[m, 8:10, :] = high[block, 6 * m + 4 : 6 * m + 6, :]
            stage[m, 14:16, :] = low[block, 6 * m : 6 * m + 2, :]
        for h in range(2):
            for e in range(4):
                ext[q * 8 + 4 * h + e, 0:24, :] = rim[a * 48 + q * 8 + 4 * h + e, 0:24, :]
            for j in range(J):
                m = (h * J + j) * 3
                for i in range(2):
                    x = [stage[m + p, 8 * i : 8 * i + 8, :] for p in range(3)]
                    x.append(fourth(x, inner))
                    at = 24 * (i + 1) + 8 * j
                    for e in range(4):
                        ext[q * 8 + 4 * h + e, at : at + 8, :] = x[e]
        return 0

    stage[...] = jnp.zeros(stage.shape, F32)
    lax.fori_loop(0, ext.shape[0] // 8, eight, 0)


def weights(rim, high, low, head, wx, wy, vv, cond, stage):
    unfold(2, rim, high, low, 0, cond, stage)
    unfold(0, rim, high, low, 6, head, stage)
    steps = head.shape[0]
    n = 3 * J
    lane = lanes((8, 128))
    sub = rows_of((8, 128))
    inner = jnp.bitwise_and(lane, 63)
    gx, gy = lax.axis_index("gx"), lax.axis_index("gy")
    last_x, last_y = lax.axis_size("gx") - 1, lax.axis_size("gy") - 1
    has = lambda there: jnp.where(there, 1.0, 0.0).astype(F32)
    beside = jnp.where(sub < 4, has(gx < last_x), has(gx > 0))
    rows = [jnp.ones((8, 128), F32), beside, beside * jnp.where((sub < 2) | (sub >= 6), 1.0, 0.0)]
    masks = []
    for i in range(3):
        for j in range(J):
            y = column(lane, j)
            in_low = jnp.where(y >= -HALO, has(gy > 0), 0.0)
            in_high = jnp.where(y < 128 + HALO, has(gy < last_y), 0.0)
            masks.append(rows[i] * jnp.where(inner < 48, jnp.where(y < 0, in_low, jnp.where(y < 128, 1.0, in_high)), 0.0))

    def known(at):
        return [jnp.where(m > 0, x, 1.0) for m, x in zip(masks, get(cond, at, n))]

    def one(at, k, inmost=False):
        k_in = swap(k) if inmost else known(at + 1)
        rock = [jnp.sqrt(x) * m for m, x in zip(masks, k)]
        put(wx, at, [time_step * a * b for a, b in zip(rock, up(rock))])
        put(wy, at, [time_step * a * b for a, b in zip(rock, nxt(rock))])
        put(vv, at, [2.0 * a * b / (a + b) for a, b in zip(k, k_in)])
        return k_in

    one(steps - 1, sweep(0, steps - 1, one, known(0), 4), True)


def prepare(rim, high, low, head, wx, wy, vv, part, side, salt, stage):
    unfold(1, rim, high, low, 0, salt, stage)
    steps = salt.shape[0]
    n = 3 * J
    weigh = tilt()

    def one(at, carry, inmost=False):
        c, lift_above = carry
        c_in = swap(c) if inmost else get(salt, at + 1, n)
        h = get(head, at, n)
        lift = [(weigh * b) * (p + q) for b, p, q in zip(get(vv, at, n), c, c_in)]
        flow, moved = sides_of(h, c, get(wx, at, n), get(wy, at, n))
        put(part, at, [a + b - p + q for a, b, p, q in zip(h, flow, lift, lift_above)])
        put(side, at, [porosity * a + b for a, b in zip(c, moved)])
        return c_in, lift

    one(steps - 1, sweep(0, steps - 1, one, (get(salt, 0, n), zeros(n)), 4), True)


def aquifer(part0, side0, salt0, wx, wy, vv, gathered, leak_high, leak_low, head_out, salt_out, hy, cz, ss, ip, uu, iq, kk, mid, leak):
    steps = salt0.shape[0]
    layers = 2 * steps
    lane = lanes((8, 128))
    inner = jnp.bitwise_and(lane, 63)
    weigh = tilt()

    leak[0:8, :] = gathered[2:10, :]
    leak[0:2, :] += leak_low[6:8, :]
    leak[6:8, :] += leak_high[0:2, :]
    leak[8:12, :] = leak_high[2:6, :]
    leak[8:10, :] += gathered[10:12, :]
    leak[12:16, :] = leak_low[2:6, :]
    leak[14:16, :] += gathered[0:2, :]
    leak[16:18, :] = leak_high[6:8, :]
    leak[18:22, :] = jnp.zeros((4, 768), F32)
    leak[22:24, :] = leak_low[0:2, :]

    def leak_of(term, n):
        out = []
        for m in range(n):
            i, j = m // J, m % J
            y = column(lane, j)
            here = leak[8 * i : 8 * i + 8, 256 * term : 256 * term + 128]
            beside = leak[8 * i : 8 * i + 8, 256 * term + 128 : 256 * term + 256]
            x = jnp.where((y >= 0) & (y < 128), take(here, jnp.clip(y, 0, 127)), take(beside, jnp.bitwise_and(y, 127)))
            out.append(jnp.where(lane < 48, x, 0.0))
        return out

    n = 3 * J
    total, level = leak_of(0, n), leak_of(1, n)

    def pivots(at, carry):
        p, q, flow = carry
        v = get(vv, at, n)
        inverse = [1.0 / (a + b) for a, b in zip(p, v)]
        u = [a * b for a, b in zip(v, inverse)]
        put(ip, at, inverse)
        put(uu, at, u)
        y = [(a + b) * i for a, b, i in zip(get(part0, at, n), flow, inverse)]
        put(hy, at, y)
        inverse = [1.0 / (a + spread_vertical * b) for a, b in zip(q, v)]
        k = [spread_vertical * a * b for a, b in zip(v, inverse)]
        put(iq, at, inverse)
        put(kk, at, k)
        return (
            [1.0 + a * (1.0 - b) for a, b in zip(v, u)],
            [porosity + spread_vertical * a * (1.0 - b) for a, b in zip(v, k)],
            [a * b for a, b in zip(v, y)],
        )

    sweep(0, steps, pivots, ([1.0 + x for x in total], [porosity + x for x in total], level))
    for place, ref in enumerate((uu, kk)):
        u = get(ref, steps - 1, n)
        put(mid, place, [1.0 / (1.0 - a * b) for a, b in zip(u, swap(u))])

    def outward(state, ratio, place, n):
        y, u = get(state, steps - 1, n), get(ratio, steps - 1, n)
        x = [(a + b * c) * d for a, b, c, d in zip(y, u, swap(y), get(mid, place, n))]
        put(state, steps - 1, x)

        def back(t, x):
            at = steps - 2 - t
            x = [a + b * c for a, b, c in zip(get(state, at, n), get(ratio, at, n), x)]
            put(state, at, x)
            return x

        sweep(0, steps - 1, back, x)

    in_order = [jnp.right_shift((lane + 8 - j) * 21846, 16) for j in range(J)]
    owner = lane + 8 - 3 * jnp.right_shift((lane + 8) * 21846, 16)

    def write(out, at, x):
        for end in range(2):
            y = [take(z, jnp.clip(index, 0, 63) + 64 * end) for z, index in zip(x, in_order)]
            layer = at if end == 0 else layers - 1 - at
            out[layer] = jnp.where(owner == 0, y[0], jnp.where(owner == 1, y[1], y[2]))

    for step in range(AQ_ITERS):
        last = step == AQ_ITERS - 1
        n_in = J * (3 if step < 2 else 2)
        n = J * (3 if step == 0 else 1 if last else 2)
        salt = salt0 if step == 0 else cz
        if step > 0:
            def inward(at, carry, n_in=n_in, n=n, inmost=False):
                c, lift_above, flow_above = carry
                c_in = swap(c) if inmost else get(cz, at + 1, n_in)
                v = get(vv, at, n)
                lift = [(weigh * b) * (p + q) for b, p, q in zip(v, c, c_in)]
                h = get(hy, at, n_in)
                flow, moved = sides_of(h, c, get(wx, at, n_in), get(wy, at, n_in))
                y = [
                    (a + b - p + q + r) * i
                    for a, b, p, q, r, i in zip(h, flow, lift, lift_above, flow_above, get(ip, at, n))
                ]
                put(hy, at, y)
                put(ss, at, [porosity * a + b for a, b in zip(c[:n], moved)])
                return c_in, lift, [a * b for a, b in zip(v, y)]

            carry = sweep(0, steps - 1, inward, (get(cz, 0, n_in), zeros(n), leak_of(1, n)))
            inward(steps - 1, carry, inmost=True)
        outward(hy, uu, 0, n)

        source = side0 if step == 0 else ss

        def salt_inward(at, carry, n=n, salt=salt, source=source, last=last, inmost=False):
            h, c, carried_above, z_above = carry
            h_in = swap(h) if inmost else get(hy, at + 1, n)
            c_in = swap(c) if inmost else get(salt, at + 1, n)
            v = get(vv, at, n)
            rising = [
                x * (time_step * (a - b) - (time_step * weigh) * (p + q))
                for x, a, b, p, q in zip(v, h_in, h, c_in, c)
            ]
            carried = [r * jnp.where(r > 0, p, q) for r, p, q in zip(rising, c_in, c)]
            z = [
                (s + a - b + y) * i
                for s, a, b, y, i in zip(get(source, at, n), carried, carried_above, z_above, get(iq, at, n))
            ]
            put(cz, at, z)
            if last:
                write(head_out, at, h)
            return h_in, c_in, carried, [spread_vertical * x * y for x, y in zip(v, z)]

        carry = sweep(0, steps - 1, salt_inward, (get(hy, 0, n), get(salt, 0, n), zeros(n), leak_of(2, n)))
        salt_inward(steps - 1, carry, inmost=True)
        outward(cz, kk, 1, n)

    sweep(0, steps, lambda at, _: write(salt_out, at, get(cz, at, J)) or 0, 0)


def whole(steps):
    return (steps, 24 * J, 128)


def run_weights(rim, high, low):
    steps = rim.shape[0] // 3
    return call(
        weights,
        [whole(steps)] * 4,
        (rim, high, low),
        "weights",
        scratch=[pltpu.VMEM(whole(steps), F32), pltpu.VMEM((18, 16, 128), F32)],
        micros=4.0,
    )


def run_prepare(rim, high, low, *ready):
    steps = rim.shape[0] // 3
    return call(
        prepare,
        [whole(steps)] * 3,
        (rim, high, low, *ready),
        "prepare",
        scratch=[pltpu.VMEM((18, 16, 128), F32)],
        micros=4.0,
    )


def run_aquifer(*args):
    steps = args[0].shape[0]
    return call(
        aquifer,
        [(2 * steps, 8, 128)] * 2,
        args,
        "aquifer",
        scratch=[pltpu.VMEM(whole(steps), F32)] * 7 + [pltpu.VMEM((2, 24 * J, 128), F32), pltpu.VMEM((24, 768), F32)],
        keep=(0, 1),
        micros=20.0,
    )


def local(surf_depth, surf_bed, surf_conv, wet_mask, surf_salt, seabed_leak, seabed_shift, active_count, aq_head, aq_salt, aq_cond):
    shifts = seabed_shift.reshape(-1, 2).T
    counts = active_count.reshape(1, -1)
    steps = aq_head.shape[0] // 2
    args = (surf_depth, surf_bed, surf_conv, wet_mask, surf_salt, seabed_leak, shifts, counts, aq_head, aq_salt, aq_cond)
    rim = (152, 128)
    in_low, in_high, rows_low, rows_high, *args = call(
        pack_inland,
        [rim, rim, (8, 128), (8, 128), *(jax.typeof(x) for x in args)],
        args,
        "pack_inland",
        scratch=[pltpu.SemaphoreType.DMA((11,))],
        raw=range(11),
        micros=3.0,
    )
    aq = args[8:]
    right = shift(in_low, "gy", -1)
    left = shift(in_high, "gy", 1)
    tiles = call(interleave, [(steps // 8, 18, 8, 128)] * 3, aq, "interleave", micros=4.0)
    join_low, join_high = call(join_rims, [(24, 128)] * 2, (right, left, rows_low, rows_high, tiles[0]), "join_rims")
    above = shift(join_low, "gx", -1)
    below = shift(join_high, "gx", 1)
    blocks = 3 * steps // 8
    full, *coast = call(
        pack_coast,
        [(blocks, 18, 8, 128)] + [(blocks // 3 * 2, 112, 128)] * 2 + [(blocks // 3, 112, 128)] * 2,
        (*tiles, right, left),
        "pack_coast",
        micros=3.0,
    )
    rims = call(open_tile, [(3 * steps, 8 * J, 128)], (full,), "open_tile", micros=3.0)[0]
    first_low, first_high = behind(coast[:2], above, below)
    first = shift(first_low, "gx", -1), shift(first_high, "gx", 1)
    depth, to_low, to_high, to_low2, to_high2, own = call(
        surface,
        [(128, 128), (32, 384), (32, 384), (16, 384), (16, 384), (16, 768)],
        (*args[:8], right, left, above, below),
        "surface",
        scratch=[pltpu.VMEM((136, 256), F32)] * 2,
        keep=(0,),
        micros=1.5,
    )
    leak_right = shift(to_low, "gy", -1)
    leak_left = shift(to_high, "gy", 1)
    leak_right2 = shift(to_low2, "gy", -2)
    leak_left2 = shift(to_high2, "gy", 2)
    then_low, then_high = behind(coast[2:], leak_right, leak_left, leak_right2, leak_left2)
    then = shift(then_low, "gx", -1), shift(then_high, "gx", 1)
    head, *links = run_weights(rims, *first)
    ready = run_prepare(rims, *then, head, *links)
    gathered, sum_low, sum_high = call(
        sum_inland, [(16, 768), (8, 768), (8, 768)], (own, leak_right, leak_left, leak_right2, leak_left2), "sum_inland"
    )
    leak_high = shift(sum_low, "gx", -1)
    leak_low = shift(sum_high, "gx", 1)
    head, salt = run_aquifer(*ready, *links, gathered, leak_high, leak_low)
    return depth, head, salt


def solution(mesh):
    in_specs = (
        P("gx", "gy"),
        P("gx", "gy"),
        P("gx", "gy"),
        P("gx", "gy"),
        P("gx", "gy"),
        P("gx", "gy"),
        P("gx", "gy", None, None),
        P("gx", "gy", None),
        P(None, "gx", "gy"),
        P(None, "gx", "gy"),
        P(None, "gx", "gy"),
    )
    out_specs = (P("gx", "gy"), P(None, "gx", "gy"), P(None, "gx", "gy"))
    return jax.shard_map(local, mesh=mesh, in_specs=in_specs, out_specs=out_specs, check_vma=False)
```

```python
import functools

import jax
import jax.numpy as jnp
from jax import lax
from jax.experimental import pallas as pl
from jax.experimental.pallas import tpu as pltpu
from jax.sharding import PartitionSpec as P

SURF_STEPS = 4
AQ_ITERS = 6
HALO = 6

surface_rate = 0.24
time_step = 0.05
density_slope = 0.025
porosity = 0.35
spread_side = 0.1
spread_vertical = 0.1

F32 = jnp.float32
VMEM_LIMIT = 20 * 2**20
UNROLL = 8
HEAD_SCALE = 10.0


def shift(block, axis, step):
    count = lax.axis_size(axis)
    return lax.ppermute(block, axis, [(i, (i + step) % count) for i in range(count)])


def call(body, outs, args, name, scratch=(), keep=(), raw=(), away=(), micros=1.0):
    outs = [x if isinstance(x, jax.core.ShapedArray) else jax.ShapeDtypeStruct(x, F32) for x in outs]
    shapes = [x if i in keep else pltpu.VMEM(x.shape, x.dtype) for i, x in enumerate(outs)]
    args = [pltpu.with_memory_space_constraint(x, pltpu.HBM) if i in raw else x for i, x in enumerate(args)]
    spec = lambda i: pl.BlockSpec(memory_space=pltpu.HBM if i in raw else pltpu.VMEM)
    return pl.pallas_call(
        body,
        out_shape=shapes,
        in_specs=[spec(i) for i in range(len(args))],
        out_specs=[pl.BlockSpec(memory_space=pltpu.HBM if i in away else pltpu.VMEM) for i in range(len(outs))],
        scratch_shapes=list(scratch),
        compiler_params=pltpu.CompilerParams(vmem_limit_bytes=VMEM_LIMIT),
        cost_estimate=pl.CostEstimate(flops=0, bytes_accessed=int(micros * 3.5e6), transcendentals=0),
        name=name,
    )(*args)


def behind(arrays, *first):
    def body(*refs):
        del refs

    count = len(arrays)
    return pl.pallas_call(
        body,
        out_shape=[pltpu.VMEM(x.shape, x.dtype) for x in arrays],
        in_specs=[pl.BlockSpec(memory_space=pltpu.VMEM)] * (count + len(first)),
        out_specs=[pl.BlockSpec(memory_space=pltpu.VMEM)] * count,
        input_output_aliases={i: i for i in range(count)},
        compiler_params=pltpu.CompilerParams(vmem_limit_bytes=VMEM_LIMIT),
        name="behind",
    )(*arrays, *first)


def lanes(shape):
    return lax.broadcasted_iota(jnp.int32, shape, len(shape) - 1)


def rows_of(shape):
    return lax.broadcasted_iota(jnp.int32, shape, len(shape) - 2)


def roll(x, by, axis):
    by = by % x.shape[axis]
    return x if by == 0 else pltpu.roll(x, by, axis)


def pack_inland(*refs):
    args, (to_low, to_high, rows_low, rows_high), here, sems = refs[:11], refs[11:15], refs[15:26], refs[26]
    copies = [pltpu.make_async_copy(x, y, sems.at[i]) for i, (x, y) in enumerate(zip(args, here))]
    surf_copies, late_copies, aq_copies = copies[:4], copies[4:8], copies[8:]
    for copy in (*surf_copies, *aq_copies, *late_copies):
        copy.start()
    for copy in surf_copies:
        copy.wait()
    depth, bed, conv, wet = here[:4]
    lane = lanes((8, 128))
    sub = rows_of((8, 128))
    level_rows, conduct_rows, tiles = [], [], []
    for t in range(16):
        at = slice(8 * t, 8 * t + 8)
        level = bed[at, :] + depth[at, :]
        conduct = wet[at, :].astype(F32) * jnp.sqrt(conv[at, :])
        level_rows.append(level)
        conduct_rows.append(conduct)
        tiles.append((jnp.where(lane < 4, level, roll(conduct, 4, 1)), jnp.where(lane < 4, roll(level, 4, 1), roll(conduct, 8, 1))))
    low, high = tiles[0]
    for t in range(1, 16):
        at = lane >= 8 * t
        low = jnp.where(at, roll(tiles[t][0], 8 * t, 1), low)
        high = jnp.where(at, roll(tiles[t][1], 8 * t, 1), high)
    to_low[144:152, :] = low
    to_high[144:152, :] = high
    rows_low[...] = jnp.where(sub < 4, level_rows[0], roll(conduct_rows[0], 4, 0))
    rows_high[...] = jnp.where(sub >= 4, level_rows[15], roll(conduct_rows[15], 4, 0))
    first = jnp.bitwise_and(lane, 8) == 0
    for a in range(3):
        aq_copies[a].wait()
        ref = here[8 + a]
        last = ref.shape[0] - 1
        for q in range(6):
            ends = []
            for h in range(2):
                t = 8 * q + 4 * h
                layers = [t + e for e in range(4)] + [last - t - e for e in range(4)]
                x = roll(ref[layers[0]], 8, 1)
                for k in range(1, 8):
                    x = jnp.where(lane >= 16 * k, roll(ref[layers[k]], 16 * k + 8, 1), x)
                ends.append(x)
            at = slice((a * 6 + q) * 8, (a * 6 + q) * 8 + 8)
            to_low[at, :] = jnp.where(first, roll(ends[1], -8, 1), ends[0])
            to_high[at, :] = jnp.where(first, ends[0], roll(ends[1], 8, 1))
    for copy in late_copies:
        copy.wait()


def join_rims(right, left, rows_low, rows_high, after, to_low, to_high):
    del after
    for out, rows in ((to_low, rows_low), (to_high, rows_high)):
        out[0:8, :] = right[144:152, :]
        out[8:16, :] = left[144:152, :]
        out[16:24, :] = rows[...]


def inside(shape, row_low, row_high, col_low, col_high):
    gx, gy = lax.axis_index("gx"), lax.axis_index("gy")
    last_x, last_y = lax.axis_size("gx") - 1, lax.axis_size("gy") - 1
    one = jnp.ones(shape, F32)
    zero = jnp.zeros(shape, F32)
    has = lambda there: jnp.where(there, 1.0, 0.0).astype(F32)
    row = jnp.where(row_high, one * has(gx < last_x), jnp.where(row_low, one * has(gx > 0), one))
    lane = lanes(shape)
    col = jnp.where(
        lane < 128,
        one,
        jnp.where(
            lane < 128 + col_high,
            one * has(gy < last_y),
            jnp.where(lane >= 256 - col_low, one * has(gy > 0), zero),
        ),
    )
    return row * col


def dot(a, b, dims):
    return lax.dot_general(a, b, (dims, ((), ())), precision=lax.Precision.HIGHEST, preferred_element_type=F32)


def surface(depth, bed, conv, wet, salt, leak, shifts, counts, right, left, above, below, depth_out, to_low, to_high, to_low2, to_high2, own, level_ref, conduct_ref):
    lane = lanes((8, 128))
    sub = rows_of((8, 128))
    ring = lanes((8, 256))
    sub_ring = rows_of((8, 256))
    column_in = inside((8, 256), sub_ring < 0, sub_ring < 0, 4, 4)
    corner_in = inside((8, 256), sub_ring >= 4, sub_ring < 4, 4, 4)

    def sides(r, l, t):
        level = jnp.where(lane < 4, roll(r, -8 * t, 1), roll(l, 124 - 8 * t, 1))
        conduct = jnp.where(lane < 4, roll(r, -8 * t - 4, 1), roll(l, 120 - 8 * t, 1))
        return level, conduct

    r, l = right[144:152, :], left[144:152, :]
    for t in range(16):
        here = slice(8 * t, 8 * t + 8)
        level, conduct = sides(r, l, t)
        level_ref[here, 0:128] = bed[here, :] + depth[here, :]
        level_ref[here, 128:256] = level
        conduct_ref[here, 0:128] = wet[here, :].astype(F32) * jnp.sqrt(conv[here, :])
        conduct_ref[here, 128:256] = conduct * column_in[:, 128:]
    high_rows, low_rows = above[16:24, :], below[16:24, :]
    high_sides = sides(above[0:8, :], above[8:16, :], 0)
    low_sides = sides(below[0:8, :], below[8:16, :], 15)
    level_ref[128:136, 0:128] = jnp.where(sub < 4, high_rows, low_rows)
    level_ref[128:136, 128:256] = jnp.where(sub < 4, high_sides[0], low_sides[0])
    conduct_ref[128:136, 0:128] = roll(jnp.where(sub >= 4, high_rows, low_rows), 4, 0) * corner_in[:, :128]
    conduct_ref[128:136, 128:256] = jnp.where(sub < 4, high_sides[1], low_sides[1]) * corner_in[:, 128:]

    level = level_ref[...]
    conduct = conduct_ref[...]
    link_x = surface_rate * conduct * roll(conduct, -1, 0)
    link_y = surface_rate * conduct * roll(conduct, -1, 1)
    final = depth[...]
    total = jnp.zeros((128, 128), F32)
    for _ in range(SURF_STEPS):
        flow_x = link_x * (roll(level, -1, 0) - level)
        flow_y = link_y * (roll(level, -1, 1) - level)
        moved = (flow_x - roll(flow_x, 1, 0)) + (flow_y - roll(flow_y, 1, 1))
        level = level + moved
        final = final + moved[0:128, 0:128]
        total = total + level[0:128, 0:128]
    depth_out[...] = final
    mean_level = total * (1.0 / SURF_STEPS)

    square = (128, 128)
    count = jnp.transpose(jnp.broadcast_to(counts[...].astype(F32), square))
    active = jnp.where(lanes(square).astype(F32) < count, 1.0, 0.0)
    cells = wet[...].astype(F32) * active * leak[...]
    gx, gy = lax.axis_index("gx"), lax.axis_index("gy")
    last_row, last_tile = 8 * lax.axis_size("gx") - 1, lax.axis_size("gy") - 1
    block = lanes((1, 128))
    global_row = gx * 128 + block + shifts[0:1, :]
    row = jnp.clip(jnp.right_shift(global_row, 4), 0, last_row) - gx * 8 + 2
    tile = jnp.clip(gy + shifts[1:2, :], 0, last_tile) - gy + 1
    target = tile * 16 + row
    choose = jnp.where(rows_of((48, 128)) == target, 1.0, 0.0)
    sums = [dot(choose, term, ((1,), (0,))) for term in (cells, cells * mean_level, cells * salt[...])]
    lane48 = lanes((16, 128))
    for i, total in enumerate(sums):
        at = slice(128 * i, 128 * i + 128)
        to_low[:, at] = total[0:32]
        to_high[:, at] = total[16:48]
        to_low2[:, at] = total[0:16]
        to_high2[:, at] = total[32:48]
        own[:, 256 * i : 256 * i + 128] = total[16:32]
        own[:, 256 * i + 128 : 256 * i + 256] = jnp.where(lane48 < 8, total[32:48], jnp.where(lane48 >= 120, total[0:16], 0.0))


def sum_inland(own, right, left, right2, left2, gathered, to_low, to_high):
    lane = lanes((16, 128))
    for i in range(3):
        at = slice(128 * i, 128 * i + 128)
        first = slice(256 * i, 256 * i + 128)
        second = slice(256 * i + 128, 256 * i + 256)
        here = own[:, first] + right[0:16, at] + left[16:32, at]
        beside = own[:, second] + jnp.where(
            lane < 8,
            right[16:32, at] + right2[:, at],
            jnp.where(lane >= 120, left[0:16, at] + left2[:, at], 0.0),
        )
        gathered[:, first] = here
        gathered[:, second] = beside
    to_low[...] = gathered[0:8, :]
    to_high[...] = gathered[4:12, :]


J = 3


def column(lane, j):
    return J * jnp.bitwise_and(lane, 63) + (j - 8)


def take(x, index):
    return jnp.take_along_axis(x, index, axis=1)


def interleave(head, salt, cond, *outs):
    lane = lanes((8, 128))
    inner = jnp.bitwise_and(lane, 63)
    index = [jnp.clip(column(lane, j), 0, 127) for j in range(J)]
    for ref, out in zip((head, salt, cond), outs):
        last = ref.shape[0] - 1

        def eight(q, _, ref=ref, out=out, last=last):
            for h in range(2):
                for j in range(J):
                    x = []
                    for e in range(4):
                        at = q * 8 + 4 * h + e
                        x.append(jnp.where(lane < 64, take(ref[at], index[j]), take(ref[last - at], index[j])))
                    m = (h * J + j) * 3
                    for p in range(3):
                        out[q, m + p] = jnp.where(inner < 48, x[p], roll(x[3], 48 - 16 * p, 1))
            return 0

        lax.fori_loop(0, (last + 1) // 16, eight, 0)


def pack_coast(head, salt, cond, right, left, full, first_low, first_high, then_low, then_high):
    lane = lanes((8, 128))
    half = jnp.bitwise_and(lane, 64)
    inner = jnp.bitwise_and(lane, 63)
    odd = jnp.bitwise_and(lane, 8) != 0
    picks = []
    for h in range(2):
        for j in range(J):
            for p in range(3):
                mine = inner < 48
                y = J * jnp.where(mine, inner, inner - 48 + 16 * p) + (j - 8)
                e = jnp.where(mine, p, 3)
                right_at, left_at = (8, 0) if h == 0 else (0, 8)
                source = 16 * e + half + jnp.where(y < 0, left_at + 8 + y, right_at + y - 128)
                picks.append(((y < 0) | (y >= 128), jnp.clip(source, 0, 127)))
    ways = ((first_low, first_high, 3), (then_low, then_high, 0), (first_low, first_high, 0))
    for a, (ref, (to_low, to_high, start)) in enumerate(zip((head, salt, cond), ways)):
        def sixteen(pair, _, a=a, ref=ref, to_low=to_low, to_high=to_high, start=start):
            for part in range(2):
                q = 2 * pair + part
                at = pl.multiple_of((a * 6 + q) * 8, 8)
                r, l = right[pl.ds(at, 8), :], left[pl.ds(at, 8), :]
                rims = (jnp.where(odd, r, l), jnp.where(odd, l, r))
                for m in range(18):
                    there, source = picks[m]
                    x = jnp.where(there, take(rims[m // 9], source), ref[q, m])
                    full[a * 6 + q, m] = x
                    row = 108 * part + 6 * m
                    to_low[start + pair, row : row + 6, :] = x[0:6]
                    to_high[start + pair, row : row + 6, :] = x[2:8]
            return 0

        lax.fori_loop(0, 3, sixteen, 0)


def fourth(x, inner):
    return jnp.where(inner < 16, roll(x[0], -48, 1), jnp.where(inner < 32, roll(x[1], -32, 1), roll(x[2], -16, 1)))


def open_tile(full, rim):
    inner = jnp.bitwise_and(lanes((8, 128)), 63)

    def eight(b, _):
        for h in range(2):
            for j in range(J):
                m = (h * J + j) * 3
                x = [full[b, m + p] for p in range(3)]
                x.append(fourth(x, inner))
                for e in range(4):
                    rim[b * 8 + 4 * h + e, 8 * j : 8 * j + 8, :] = x[e]
        return 0

    lax.fori_loop(0, 18, eight, 0)


def up(t):
    s = rows_of((8, 128))
    out = [None] * len(t)
    for j in range(J):
        x = t[j::J]
        r = [roll(y, -1, 0) for y in x]
        if len(x) == 2:
            new = [jnp.where(s == 7, r[1], r[0]), jnp.where(s == 7, r[0], r[1])]
        else:
            new = [
                jnp.where(s == 7, r[1], r[0]),
                jnp.where(s == 7, r[0], jnp.where(s == 3, roll(x[2], 3, 0), r[1])),
                jnp.where(s == 7, roll(x[1], 3, 0), r[2]),
            ]
        out[j::J] = new
    return out


def down(t):
    s = rows_of((8, 128))
    out = [None] * len(t)
    for j in range(J):
        x = t[j::J]
        r = [roll(y, 1, 0) for y in x]
        if len(x) == 2:
            new = [jnp.where(s == 0, r[1], r[0]), jnp.where(s == 0, r[0], r[1])]
        else:
            new = [
                jnp.where(s == 0, r[1], r[0]),
                jnp.where(s == 0, r[0], jnp.where(s == 4, roll(x[2], 5, 0), r[1])),
                jnp.where(s == 0, roll(x[1], 5, 0), r[2]),
            ]
        out[j::J] = new
    return out


def nxt(t):
    return [y for i in range(0, len(t), J) for y in (t[i + 1], t[i + 2], roll(t[i], -1, 1))]


def prv(t):
    return [y for i in range(0, len(t), J) for y in (roll(t[i + 2], 1, 1), t[i], t[i + 1])]


def swap(t):
    return [roll(x, 64, 1) for x in t]


def sides_of(h, c, wx, wy):
    flow = salt = None
    for w, ahead, back in ((wx, up, down), (wy, nxt, prv)):
        hs, cs = ahead(h), ahead(c)
        f, g = [], []
        for i in range(len(h)):
            dh = hs[i] - h[i]
            moved = dh * jnp.where(dh > 0, cs[i], c[i]) + (cs[i] - c[i])
            f.append(w[i] * dh)
            g.append(w[i] * moved)
        fb, gb = back(f), back(g)
        f = [a - b for a, b in zip(f, fb)]
        g = [a - b for a, b in zip(g, gb)]
        flow = f if flow is None else [a + b for a, b in zip(flow, f)]
        salt = g if salt is None else [a + b for a, b in zip(salt, g)]
    return flow, salt


def get(ref, at, n):
    return [ref[at, 8 * m : 8 * m + 8, :] for m in range(n)]


def put(ref, at, values):
    for m, x in enumerate(values):
        ref[at, 8 * m : 8 * m + 8, :] = x


def sweep(first, count, body, carry, unroll=None):
    unroll = unroll or UNROLL
    turns = count // unroll

    def turn(t, carry):
        for i in range(unroll):
            carry = body(first + t * unroll + i, carry)
        return carry

    carry = lax.fori_loop(0, turns, turn, carry)
    for i in range(turns * unroll, count):
        carry = body(first + i, carry)
    return carry


def zeros(n):
    return [jnp.zeros((8, 128), F32)] * n


def scaled(t):
    return [HEAD_SCALE * x for x in t]


def tilt():
    size = 0.5 * HEAD_SCALE * density_slope
    return jnp.where(lanes((8, 128)) < 64, size, -size).astype(F32)


def unfold(a, rim, high, low, start, ext, stage):
    inner = jnp.bitwise_and(lanes((8, 128)), 63)

    def eight(q, pair, part):
        block = start + pair
        first = 108 * part
        for m in range(18):
            stage[m, 0:4, :] = high[block, first + 6 * m : first + 6 * m + 4, :]
            stage[m, 4:8, :] = low[block, first + 6 * m + 2 : first + 6 * m + 6, :]
            stage[m, 8:10, :] = high[block, first + 6 * m + 4 : first + 6 * m + 6, :]
            stage[m, 14:16, :] = low[block, first + 6 * m : first + 6 * m + 2, :]
        for h in range(2):
            for e in range(4):
                ext[q * 8 + 4 * h + e, 0:24, :] = rim[a * 48 + q * 8 + 4 * h + e, 0:24, :]
            for j in range(J):
                m = (h * J + j) * 3
                for i in range(2):
                    x = [stage[m + p, 8 * i : 8 * i + 8, :] for p in range(3)]
                    x.append(fourth(x, inner))
                    at = 24 * (i + 1) + 8 * j
                    for e in range(4):
                        ext[q * 8 + 4 * h + e, at : at + 8, :] = x[e]

    def sixteen(pair, _):
        for part in range(2):
            eight(2 * pair + part, pair, part)
        return 0

    stage[...] = jnp.zeros(stage.shape, F32)
    lax.fori_loop(0, ext.shape[0] // 16, sixteen, 0)


def weights(rim, high, low, head, wx, wy, vv, cond, stage):
    unfold(2, rim, high, low, 0, cond, stage)
    unfold(0, rim, high, low, 3, head, stage)
    steps = head.shape[0]
    n = 3 * J
    lane = lanes((8, 128))
    sub = rows_of((8, 128))
    inner = jnp.bitwise_and(lane, 63)
    gx, gy = lax.axis_index("gx"), lax.axis_index("gy")
    last_x, last_y = lax.axis_size("gx") - 1, lax.axis_size("gy") - 1
    has = lambda there: jnp.where(there, 1.0, 0.0).astype(F32)
    beside = jnp.where(sub < 4, has(gx < last_x), has(gx > 0))
    rows = [jnp.ones((8, 128), F32), beside, beside * jnp.where((sub < 2) | (sub >= 6), 1.0, 0.0)]
    masks = []
    for i in range(3):
        for j in range(J):
            y = column(lane, j)
            in_low = jnp.where(y >= -HALO, has(gy > 0), 0.0)
            in_high = jnp.where(y < 128 + HALO, has(gy < last_y), 0.0)
            masks.append(rows[i] * jnp.where(inner < 48, jnp.where(y < 0, in_low, jnp.where(y < 128, 1.0, in_high)), 0.0))

    def known(at):
        return [jnp.where(m > 0, x, 1.0) for m, x in zip(masks, get(cond, at, n))]

    def one(at, k, inmost=False):
        k_in = swap(k) if inmost else known(at + 1)
        rock = [jnp.sqrt(x) * m for m, x in zip(masks, k)]
        put(wx, at, [time_step * a * b for a, b in zip(rock, up(rock))])
        put(wy, at, [time_step * a * b for a, b in zip(rock, nxt(rock))])
        put(vv, at, [2.0 * a * b / (a + b) for a, b in zip(k, k_in)])
        return k_in

    one(steps - 1, sweep(0, steps - 1, one, known(0), 4), True)


def prepare(rim, high, low, head, wx, wy, vv, part, side, salt, stage):
    unfold(1, rim, high, low, 0, salt, stage)
    steps = salt.shape[0]
    n = 3 * J
    weigh = tilt()

    def one(at, carry, inmost=False):
        c, lift_above = carry
        c_in = swap(c) if inmost else get(salt, at + 1, n)
        h = scaled(get(head, at, n))
        lift = [(weigh * b) * (p + q) for b, p, q in zip(get(vv, at, n), c, c_in)]
        flow, moved = sides_of(h, c, get(wx, at, n), get(wy, at, n))
        put(part, at, [a + b - p + q for a, b, p, q in zip(h, flow, lift, lift_above)])
        put(side, at, [HEAD_SCALE * porosity * a + b for a, b in zip(c, moved)])
        return c_in, lift

    one(steps - 1, sweep(0, steps - 1, one, (get(salt, 0, n), zeros(n)), 4), True)


def aquifer(part0, side0, salt0, wx, wy, vv, gathered, leak_high, leak_low, head_to, salt_to, hy, cz, ss, ip, uu, iq, kk, mid, leak, head_out, salt_out, sems):
    steps = salt0.shape[0]
    layers = 2 * steps
    lane = lanes((8, 128))
    inner = jnp.bitwise_and(lane, 63)
    weigh = tilt()

    leak[0:8, :] = gathered[2:10, :]
    leak[0:2, :] += leak_low[6:8, :]
    leak[6:8, :] += leak_high[0:2, :]
    leak[8:12, :] = leak_high[2:6, :]
    leak[8:10, :] += gathered[10:12, :]
    leak[12:16, :] = leak_low[2:6, :]
    leak[14:16, :] += gathered[0:2, :]
    leak[16:18, :] = leak_high[6:8, :]
    leak[18:22, :] = jnp.zeros((4, 768), F32)
    leak[22:24, :] = leak_low[0:2, :]

    def leak_of(term, n):
        out = []
        for m in range(n):
            i, j = m // J, m % J
            y = column(lane, j)
            here = leak[8 * i : 8 * i + 8, 256 * term : 256 * term + 128]
            beside = leak[8 * i : 8 * i + 8, 256 * term + 128 : 256 * term + 256]
            x = jnp.where((y >= 0) & (y < 128), take(here, jnp.clip(y, 0, 127)), take(beside, jnp.bitwise_and(y, 127)))
            out.append(jnp.where(lane < 48, x, 0.0))
        return out

    n = 3 * J
    total, level = leak_of(0, n), scaled(leak_of(1, n))

    def pivots(at, carry):
        p, q, flow = carry
        v = get(vv, at, n)
        inverse = [1.0 / (a + b) for a, b in zip(p, v)]
        u = [a * b for a, b in zip(v, inverse)]
        put(ip, at, inverse)
        put(uu, at, u)
        y = [(a + b) * i for a, b, i in zip(get(part0, at, n), flow, inverse)]
        put(hy, at, y)
        inverse = [1.0 / (a + b) for a, b in zip(q, v)]
        k = [a * b for a, b in zip(v, inverse)]
        put(iq, at, inverse)
        put(kk, at, k)
        return (
            [1.0 + a * (1.0 - b) for a, b in zip(v, u)],
            [HEAD_SCALE * porosity + a * (1.0 - b) for a, b in zip(v, k)],
            [a * b for a, b in zip(v, y)],
        )

    sweep(0, steps, pivots, ([1.0 + x for x in total], [HEAD_SCALE * porosity + HEAD_SCALE * x for x in total], level))
    for place, ref in enumerate((uu, kk)):
        u = get(ref, steps - 1, n)
        put(mid, place, [1.0 / (1.0 - a * b) for a, b in zip(u, swap(u))])

    in_order = [jnp.right_shift((lane + 8 - j) * 21846, 16) for j in range(J)]
    owner = lane + 8 - 3 * jnp.right_shift((lane + 8) * 21846, 16)

    def write(out, at, x):
        for end in range(2):
            y = [take(z, jnp.clip(index, 0, 63) + 64 * end) for z, index in zip(x, in_order)]
            layer = at if end == 0 else layers - 1 - at
            out[layer] = jnp.where(owner == 0, y[0], jnp.where(owner == 1, y[1], y[2]))

    def outward(state, ratio, place, n, out=None):
        y, u = get(state, steps - 1, n), get(ratio, steps - 1, n)
        x = [(a + b * c) * d for a, b, c, d in zip(y, u, swap(y), get(mid, place, n))]
        put(state, steps - 1, x)
        if out is not None:
            write(out, steps - 1, x)

        def back(t, x):
            at = steps - 2 - t
            x = [a + b * c for a, b, c in zip(get(state, at, n), get(ratio, at, n), x)]
            if out is None:
                put(state, at, x)
            else:
                write(out, at, x)
            return x

        sweep(0, steps - 1, back, x, steps - 1)

    for step in range(AQ_ITERS):
        last = step == AQ_ITERS - 1
        n_in = J * (3 if step < 2 else 2)
        n = J * (3 if step == 0 else 1 if last else 2)
        salt = salt0 if step == 0 else cz
        if step > 0:
            def inward(at, carry, n_in=n_in, n=n, inmost=False):
                c, lift_above, flow_above = carry
                c_in = swap(c) if inmost else get(cz, at + 1, n_in)
                v = get(vv, at, n)
                lift = [(weigh * b) * (p + q) for b, p, q in zip(v, c, c_in)]
                h = get(hy, at, n_in)
                flow, moved = sides_of(h, c, get(wx, at, n_in), get(wy, at, n_in))
                y = [
                    (a + b - p + q + r) * i
                    for a, b, p, q, r, i in zip(h, flow, lift, lift_above, flow_above, get(ip, at, n))
                ]
                put(hy, at, y)
                put(ss, at, [HEAD_SCALE * porosity * a + b for a, b in zip(c[:n], moved)])
                return c_in, lift, [a * b for a, b in zip(v, y)]

            carry = sweep(0, steps - 1, inward, (get(cz, 0, n_in), zeros(n), scaled(leak_of(1, n))))
            inward(steps - 1, carry, inmost=True)
        outward(hy, uu, 0, n)

        source = side0 if step == 0 else ss

        def salt_inward(at, carry, n=n, salt=salt, source=source, last=last, inmost=False):
            h, c, carried_above, z_above = carry
            h_in = swap(h) if inmost else get(hy, at + 1, n)
            c_in = swap(c) if inmost else get(salt, at + 1, n)
            v = get(vv, at, n)
            rising = [
                x * (time_step * (a - b) - (time_step * weigh) * (p + q))
                for x, a, b, p, q in zip(v, h_in, h, c_in, c)
            ]
            carried = [r * jnp.where(r > 0, p, q) for r, p, q in zip(rising, c_in, c)]
            z = [
                (s + a - b + y) * i
                for s, a, b, y, i in zip(get(source, at, n), carried, carried_above, z_above, get(iq, at, n))
            ]
            put(cz, at, z)
            if last:
                write(head_out, at, [spread_side * x for x in h])
            return h_in, c_in, carried, [x * y for x, y in zip(v, z)]

        carry = sweep(0, steps - 1, salt_inward, (get(hy, 0, n), get(salt, 0, n), zeros(n), scaled(leak_of(2, n))), 16)
        salt_inward(steps - 1, carry, inmost=True)
        if last:
            head_copy = pltpu.make_async_copy(head_out, head_to, sems.at[0])
            head_copy.start()
        outward(cz, kk, 1, n, salt_out if last else None)
    salt_copy = pltpu.make_async_copy(salt_out, salt_to, sems.at[1])
    salt_copy.start()
    head_copy.wait()
    salt_copy.wait()


def whole(steps):
    return (steps, 24 * J, 128)


def run_weights(rim, high, low):
    steps = rim.shape[0] // 3
    return call(
        weights,
        [whole(steps)] * 4,
        (rim, high, low),
        "weights",
        scratch=[pltpu.VMEM(whole(steps), F32), pltpu.VMEM((18, 16, 128), F32)],
        micros=4.0,
    )


def run_prepare(rim, high, low, *ready):
    steps = rim.shape[0] // 3
    return call(
        prepare,
        [whole(steps)] * 3,
        (rim, high, low, *ready),
        "prepare",
        scratch=[pltpu.VMEM((18, 16, 128), F32)],
        micros=4.0,
    )


def run_aquifer(*args):
    steps = args[0].shape[0]
    return call(
        aquifer,
        [(2 * steps, 8, 128)] * 2,
        args,
        "aquifer",
        scratch=[pltpu.VMEM(whole(steps), F32)] * 7 + [pltpu.VMEM((2, 24 * J, 128), F32), pltpu.VMEM((24, 768), F32)]
        + [pltpu.VMEM((2 * steps, 8, 128), F32)] * 2
        + [pltpu.SemaphoreType.DMA((2,))],
        keep=(0, 1),
        away=(0, 1),
        micros=20.0,
    )


def local(surf_depth, surf_bed, surf_conv, wet_mask, surf_salt, seabed_leak, seabed_shift, active_count, aq_head, aq_salt, aq_cond):
    shifts = seabed_shift.reshape(-1, 2).T
    counts = active_count.reshape(1, -1)
    steps = aq_head.shape[0] // 2
    args = (surf_depth, surf_bed, surf_conv, wet_mask, surf_salt, seabed_leak, shifts, counts, aq_head, aq_salt, aq_cond)
    rim = (152, 128)
    in_low, in_high, rows_low, rows_high, *args = call(
        pack_inland,
        [rim, rim, (8, 128), (8, 128), *(jax.typeof(x) for x in args)],
        args,
        "pack_inland",
        scratch=[pltpu.SemaphoreType.DMA((11,))],
        raw=range(11),
        micros=3.0,
    )
    aq = args[8:]
    right = shift(in_low, "gy", -1)
    left = shift(in_high, "gy", 1)
    tiles = call(interleave, [(steps // 8, 18, 8, 128)] * 3, aq, "interleave", micros=4.0)
    join_low, join_high = call(join_rims, [(24, 128)] * 2, (right, left, rows_low, rows_high, tiles[0]), "join_rims")
    above = shift(join_low, "gx", -1)
    below = shift(join_high, "gx", 1)
    blocks = 3 * steps // 8
    full, *coast = call(
        pack_coast,
        [(blocks, 18, 8, 128)] + [(blocks // 3, 216, 128)] * 2 + [(blocks // 6, 216, 128)] * 2,
        (*tiles, right, left),
        "pack_coast",
        micros=3.0,
    )
    rims = call(open_tile, [(3 * steps, 8 * J, 128)], (full,), "open_tile", micros=3.0)[0]
    first_low, first_high = behind(coast[:2], above, below)
    first = shift(first_low, "gx", -1), shift(first_high, "gx", 1)
    depth, to_low, to_high, to_low2, to_high2, own = call(
        surface,
        [(128, 128), (32, 384), (32, 384), (16, 384), (16, 384), (16, 768)],
        (*args[:8], right, left, above, below),
        "surface",
        scratch=[pltpu.VMEM((136, 256), F32)] * 2,
        keep=(0,),
        micros=1.5,
    )
    leak_right = shift(to_low, "gy", -1)
    leak_left = shift(to_high, "gy", 1)
    leak_right2 = shift(to_low2, "gy", -2)
    leak_left2 = shift(to_high2, "gy", 2)
    then_low, then_high = behind(coast[2:], leak_right, leak_left, leak_right2, leak_left2, rims)
    then = shift(then_low, "gx", -1), shift(then_high, "gx", 1)
    head, *links = run_weights(rims, *first)
    ready = run_prepare(rims, *then, head, *links)
    gathered, sum_low, sum_high = call(
        sum_inland, [(16, 768), (8, 768), (8, 768)], (own, leak_right, leak_left, leak_right2, leak_left2), "sum_inland"
    )
    leak_high = shift(sum_low, "gx", -1)
    leak_low = shift(sum_high, "gx", 1)
    head, salt = run_aquifer(*ready, *links, gathered, leak_high, leak_low)
    return depth, head, salt


def solution(mesh):
    in_specs = (
        P("gx", "gy"),
        P("gx", "gy"),
        P("gx", "gy"),
        P("gx", "gy"),
        P("gx", "gy"),
        P("gx", "gy"),
        P("gx", "gy", None, None),
        P("gx", "gy", None),
        P(None, "gx", "gy"),
        P(None, "gx", "gy"),
        P(None, "gx", "gy"),
    )
    out_specs = (P("gx", "gy"), P(None, "gx", "gy"), P(None, "gx", "gy"))
    return jax.shard_map(local, mesh=mesh, in_specs=in_specs, out_specs=out_specs, check_vma=False)
```

```python
import functools

import jax
import jax.numpy as jnp
from jax import lax
from jax.experimental import pallas as pl
from jax.experimental.pallas import tpu as pltpu
from jax.sharding import PartitionSpec as P

SURF_STEPS = 4
AQ_ITERS = 6
HALO = 6

surface_rate = 0.24
time_step = 0.05
density_slope = 0.025
porosity = 0.35
spread_side = 0.1
spread_vertical = 0.1

F32 = jnp.float32
VMEM_LIMIT = 20 * 2**20
UNROLL = 8
HEAD_SCALE = 10.0


def shift(block, axis, step):
    count = lax.axis_size(axis)
    return lax.ppermute(block, axis, [(i, (i + step) % count) for i in range(count)])


def call(body, outs, args, name, scratch=(), keep=(), raw=(), away=(), micros=1.0):
    outs = [x if isinstance(x, jax.core.ShapedArray) else jax.ShapeDtypeStruct(x, F32) for x in outs]
    shapes = [x if i in keep else pltpu.VMEM(x.shape, x.dtype) for i, x in enumerate(outs)]
    args = [pltpu.with_memory_space_constraint(x, pltpu.HBM) if i in raw else x for i, x in enumerate(args)]
    spec = lambda i: pl.BlockSpec(memory_space=pltpu.HBM if i in raw else pltpu.VMEM)
    return pl.pallas_call(
        body,
        out_shape=shapes,
        in_specs=[spec(i) for i in range(len(args))],
        out_specs=[pl.BlockSpec(memory_space=pltpu.HBM if i in away else pltpu.VMEM) for i in range(len(outs))],
        scratch_shapes=list(scratch),
        compiler_params=pltpu.CompilerParams(vmem_limit_bytes=VMEM_LIMIT),
        cost_estimate=pl.CostEstimate(flops=0, bytes_accessed=int(micros * 3.5e6), transcendentals=0),
        name=name,
    )(*args)


def behind(arrays, *first):
    def body(*refs):
        del refs

    count = len(arrays)
    return pl.pallas_call(
        body,
        out_shape=[pltpu.VMEM(x.shape, x.dtype) for x in arrays],
        in_specs=[pl.BlockSpec(memory_space=pltpu.VMEM)] * (count + len(first)),
        out_specs=[pl.BlockSpec(memory_space=pltpu.VMEM)] * count,
        input_output_aliases={i: i for i in range(count)},
        compiler_params=pltpu.CompilerParams(vmem_limit_bytes=VMEM_LIMIT),
        name="behind",
    )(*arrays, *first)


def lanes(shape):
    return lax.broadcasted_iota(jnp.int32, shape, len(shape) - 1)


def rows_of(shape):
    return lax.broadcasted_iota(jnp.int32, shape, len(shape) - 2)


def roll(x, by, axis):
    by = by % x.shape[axis]
    return x if by == 0 else pltpu.roll(x, by, axis)


def pack_inland(*refs):
    args, (to_low, to_high, rows_low, rows_high), here, sems = refs[:11], refs[11:15], refs[15:26], refs[26]
    copies = [pltpu.make_async_copy(x, y, sems.at[i]) for i, (x, y) in enumerate(zip(args, here))]
    surf_copies, late_copies, aq_copies = copies[:4], copies[4:8], copies[8:]
    for copy in (*surf_copies, *aq_copies, *late_copies):
        copy.start()
    for copy in surf_copies:
        copy.wait()
    depth, bed, conv, wet = here[:4]
    lane = lanes((8, 128))
    sub = rows_of((8, 128))
    level_rows, conduct_rows, tiles = [], [], []
    for t in range(16):
        at = slice(8 * t, 8 * t + 8)
        level = bed[at, :] + depth[at, :]
        conduct = wet[at, :].astype(F32) * jnp.sqrt(conv[at, :])
        level_rows.append(level)
        conduct_rows.append(conduct)
        tiles.append((jnp.where(lane < 4, level, roll(conduct, 4, 1)), jnp.where(lane < 4, roll(level, 4, 1), roll(conduct, 8, 1))))
    low, high = tiles[0]
    for t in range(1, 16):
        at = lane >= 8 * t
        low = jnp.where(at, roll(tiles[t][0], 8 * t, 1), low)
        high = jnp.where(at, roll(tiles[t][1], 8 * t, 1), high)
    to_low[144:152, :] = low
    to_high[144:152, :] = high
    rows_low[...] = jnp.where(sub < 4, level_rows[0], roll(conduct_rows[0], 4, 0))
    rows_high[...] = jnp.where(sub >= 4, level_rows[15], roll(conduct_rows[15], 4, 0))
    first = jnp.bitwise_and(lane, 8) == 0
    for a in range(3):
        aq_copies[a].wait()
        ref = here[8 + a]
        last = ref.shape[0] - 1
        for q in range(6):
            ends = []
            for h in range(2):
                t = 8 * q + 4 * h
                layers = [t + e for e in range(4)] + [last - t - e for e in range(4)]
                x = roll(ref[layers[0]], 8, 1)
                for k in range(1, 8):
                    x = jnp.where(lane >= 16 * k, roll(ref[layers[k]], 16 * k + 8, 1), x)
                ends.append(x)
            at = slice((a * 6 + q) * 8, (a * 6 + q) * 8 + 8)
            to_low[at, :] = jnp.where(first, roll(ends[1], -8, 1), ends[0])
            to_high[at, :] = jnp.where(first, ends[0], roll(ends[1], 8, 1))
    for copy in late_copies:
        copy.wait()


def join_rims(right, left, rows_low, rows_high, after, to_low, to_high):
    del after
    for out, rows in ((to_low, rows_low), (to_high, rows_high)):
        out[0:8, :] = right[144:152, :]
        out[8:16, :] = left[144:152, :]
        out[16:24, :] = rows[...]


def inside(shape, row_low, row_high, col_low, col_high):
    gx, gy = lax.axis_index("gx"), lax.axis_index("gy")
    last_x, last_y = lax.axis_size("gx") - 1, lax.axis_size("gy") - 1
    one = jnp.ones(shape, F32)
    zero = jnp.zeros(shape, F32)
    has = lambda there: jnp.where(there, 1.0, 0.0).astype(F32)
    row = jnp.where(row_high, one * has(gx < last_x), jnp.where(row_low, one * has(gx > 0), one))
    lane = lanes(shape)
    col = jnp.where(
        lane < 128,
        one,
        jnp.where(
            lane < 128 + col_high,
            one * has(gy < last_y),
            jnp.where(lane >= 256 - col_low, one * has(gy > 0), zero),
        ),
    )
    return row * col


def dot(a, b, dims):
    return lax.dot_general(a, b, (dims, ((), ())), precision=lax.Precision.HIGHEST, preferred_element_type=F32)


def surface(depth, bed, conv, wet, salt, leak, shifts, counts, right, left, above, below, depth_out, to_low, to_high, to_low2, to_high2, own, level_ref, conduct_ref):
    lane = lanes((8, 128))
    sub = rows_of((8, 128))
    ring = lanes((8, 256))
    sub_ring = rows_of((8, 256))
    column_in = inside((8, 256), sub_ring < 0, sub_ring < 0, 4, 4)
    corner_in = inside((8, 256), sub_ring >= 4, sub_ring < 4, 4, 4)

    def sides(r, l, t):
        level = jnp.where(lane < 4, roll(r, -8 * t, 1), roll(l, 124 - 8 * t, 1))
        conduct = jnp.where(lane < 4, roll(r, -8 * t - 4, 1), roll(l, 120 - 8 * t, 1))
        return level, conduct

    r, l = right[144:152, :], left[144:152, :]
    for t in range(16):
        here = slice(8 * t, 8 * t + 8)
        level, conduct = sides(r, l, t)
        level_ref[here, 0:128] = bed[here, :] + depth[here, :]
        level_ref[here, 128:256] = level
        conduct_ref[here, 0:128] = wet[here, :].astype(F32) * jnp.sqrt(conv[here, :])
        conduct_ref[here, 128:256] = conduct * column_in[:, 128:]
    high_rows, low_rows = above[16:24, :], below[16:24, :]
    high_sides = sides(above[0:8, :], above[8:16, :], 0)
    low_sides = sides(below[0:8, :], below[8:16, :], 15)
    level_ref[128:136, 0:128] = jnp.where(sub < 4, high_rows, low_rows)
    level_ref[128:136, 128:256] = jnp.where(sub < 4, high_sides[0], low_sides[0])
    conduct_ref[128:136, 0:128] = roll(jnp.where(sub >= 4, high_rows, low_rows), 4, 0) * corner_in[:, :128]
    conduct_ref[128:136, 128:256] = jnp.where(sub < 4, high_sides[1], low_sides[1]) * corner_in[:, 128:]

    level = level_ref[...]
    conduct = conduct_ref[...]
    link_x = surface_rate * conduct * roll(conduct, -1, 0)
    link_y = surface_rate * conduct * roll(conduct, -1, 1)
    final = depth[...]
    total = jnp.zeros((128, 128), F32)
    for _ in range(SURF_STEPS):
        flow_x = link_x * (roll(level, -1, 0) - level)
        flow_y = link_y * (roll(level, -1, 1) - level)
        moved = (flow_x - roll(flow_x, 1, 0)) + (flow_y - roll(flow_y, 1, 1))
        level = level + moved
        final = final + moved[0:128, 0:128]
        total = total + level[0:128, 0:128]
    depth_out[...] = final
    mean_level = total * (1.0 / SURF_STEPS)

    square = (128, 128)
    count = jnp.transpose(jnp.broadcast_to(counts[...].astype(F32), square))
    active = jnp.where(lanes(square).astype(F32) < count, 1.0, 0.0)
    cells = wet[...].astype(F32) * active * leak[...]
    gx, gy = lax.axis_index("gx"), lax.axis_index("gy")
    last_row, last_tile = 8 * lax.axis_size("gx") - 1, lax.axis_size("gy") - 1
    block = lanes((1, 128))
    global_row = gx * 128 + block + shifts[0:1, :]
    row = jnp.clip(jnp.right_shift(global_row, 4), 0, last_row) - gx * 8 + 2
    tile = jnp.clip(gy + shifts[1:2, :], 0, last_tile) - gy + 1
    target = tile * 16 + row
    choose = jnp.where(rows_of((48, 128)) == target, 1.0, 0.0)
    sums = [dot(choose, term, ((1,), (0,))) for term in (cells, cells * mean_level, cells * salt[...])]
    lane48 = lanes((16, 128))
    for i, total in enumerate(sums):
        at = slice(128 * i, 128 * i + 128)
        to_low[:, at] = total[0:32]
        to_high[:, at] = total[16:48]
        to_low2[:, at] = total[0:16]
        to_high2[:, at] = total[32:48]
        own[:, 256 * i : 256 * i + 128] = total[16:32]
        own[:, 256 * i + 128 : 256 * i + 256] = jnp.where(lane48 < 8, total[32:48], jnp.where(lane48 >= 120, total[0:16], 0.0))


def sum_inland(own, right, left, right2, left2, gathered, to_low, to_high):
    lane = lanes((16, 128))
    for i in range(3):
        at = slice(128 * i, 128 * i + 128)
        first = slice(256 * i, 256 * i + 128)
        second = slice(256 * i + 128, 256 * i + 256)
        here = own[:, first] + right[0:16, at] + left[16:32, at]
        beside = own[:, second] + jnp.where(
            lane < 8,
            right[16:32, at] + right2[:, at],
            jnp.where(lane >= 120, left[0:16, at] + left2[:, at], 0.0),
        )
        gathered[:, first] = here
        gathered[:, second] = beside
    to_low[...] = gathered[0:8, :]
    to_high[...] = gathered[4:12, :]


J = 3


def column(lane, j):
    return J * jnp.bitwise_and(lane, 63) + (j - 8)


def take(x, index):
    return jnp.take_along_axis(x, index, axis=1)


def interleave(head, salt, cond, *outs):
    lane = lanes((8, 128))
    inner = jnp.bitwise_and(lane, 63)
    index = [jnp.clip(column(lane, j), 0, 127) for j in range(J)]
    for ref, out in zip((head, salt, cond), outs):
        last = ref.shape[0] - 1

        def eight(q, _, ref=ref, out=out, last=last):
            for h in range(2):
                for j in range(J):
                    x = []
                    for e in range(4):
                        at = q * 8 + 4 * h + e
                        x.append(jnp.where(lane < 64, take(ref[at], index[j]), take(ref[last - at], index[j])))
                    m = (h * J + j) * 3
                    for p in range(3):
                        out[q, m + p] = jnp.where(inner < 48, x[p], roll(x[3], 48 - 16 * p, 1))
            return 0

        lax.fori_loop(0, (last + 1) // 16, eight, 0)


def pack_coast(head, salt, cond, right, left, full, first_low, first_high, then_low, then_high):
    lane = lanes((8, 128))
    half = jnp.bitwise_and(lane, 64)
    inner = jnp.bitwise_and(lane, 63)
    odd = jnp.bitwise_and(lane, 8) != 0
    picks = []
    for h in range(2):
        for j in range(J):
            for p in range(3):
                mine = inner < 48
                y = J * jnp.where(mine, inner, inner - 48 + 16 * p) + (j - 8)
                e = jnp.where(mine, p, 3)
                right_at, left_at = (8, 0) if h == 0 else (0, 8)
                source = 16 * e + half + jnp.where(y < 0, left_at + 8 + y, right_at + y - 128)
                picks.append(((y < 0) | (y >= 128), jnp.clip(source, 0, 127)))
    ways = ((first_low, first_high, 3), (then_low, then_high, 0), (first_low, first_high, 0))
    for a, (ref, (to_low, to_high, start)) in enumerate(zip((head, salt, cond), ways)):
        def sixteen(pair, _, a=a, ref=ref, to_low=to_low, to_high=to_high, start=start):
            for part in range(2):
                q = 2 * pair + part
                at = pl.multiple_of((a * 6 + q) * 8, 8)
                r, l = right[pl.ds(at, 8), :], left[pl.ds(at, 8), :]
                rims = (jnp.where(odd, r, l), jnp.where(odd, l, r))
                for m in range(18):
                    there, source = picks[m]
                    x = jnp.where(there, take(rims[m // 9], source), ref[q, m])
                    full[a * 6 + q, m] = x
                    row = 108 * part + 6 * m
                    to_low[start + pair, row : row + 6, :] = x[0:6]
                    to_high[start + pair, row : row + 6, :] = x[2:8]
            return 0

        lax.fori_loop(0, 3, sixteen, 0)


def fourth(x, inner):
    return jnp.where(inner < 16, roll(x[0], -48, 1), jnp.where(inner < 32, roll(x[1], -32, 1), roll(x[2], -16, 1)))


def open_tile(full, rim):
    inner = jnp.bitwise_and(lanes((8, 128)), 63)

    def eight(b, _):
        for h in range(2):
            for j in range(J):
                m = (h * J + j) * 3
                x = [full[b, m + p] for p in range(3)]
                x.append(fourth(x, inner))
                for e in range(4):
                    rim[b * 8 + 4 * h + e, 8 * j : 8 * j + 8, :] = x[e]
        return 0

    lax.fori_loop(0, 18, eight, 0)


def up(t):
    s = rows_of((8, 128))
    out = [None] * len(t)
    for j in range(J):
        x = t[j::J]
        r = [roll(y, -1, 0) for y in x]
        if len(x) == 2:
            new = [jnp.where(s == 7, r[1], r[0]), jnp.where(s == 7, r[0], r[1])]
        else:
            new = [
                jnp.where(s == 7, r[1], r[0]),
                jnp.where(s == 7, r[0], jnp.where(s == 3, roll(x[2], 3, 0), r[1])),
                jnp.where(s == 7, roll(x[1], 3, 0), r[2]),
            ]
        out[j::J] = new
    return out


def down(t):
    s = rows_of((8, 128))
    out = [None] * len(t)
    for j in range(J):
        x = t[j::J]
        r = [roll(y, 1, 0) for y in x]
        if len(x) == 2:
            new = [jnp.where(s == 0, r[1], r[0]), jnp.where(s == 0, r[0], r[1])]
        else:
            new = [
                jnp.where(s == 0, r[1], r[0]),
                jnp.where(s == 0, r[0], jnp.where(s == 4, roll(x[2], 5, 0), r[1])),
                jnp.where(s == 0, roll(x[1], 5, 0), r[2]),
            ]
        out[j::J] = new
    return out


def nxt(t):
    return [y for i in range(0, len(t), J) for y in (t[i + 1], t[i + 2], roll(t[i], -1, 1))]


def prv(t):
    return [y for i in range(0, len(t), J) for y in (roll(t[i + 2], 1, 1), t[i], t[i + 1])]


def swap(t):
    return [roll(x, 64, 1) for x in t]


def sides_of(h, c, wx, wy):
    flow = salt = None
    for w, ahead, back in ((wx, up, down), (wy, nxt, prv)):
        hs, cs = ahead(h), ahead(c)
        f, g = [], []
        for i in range(len(h)):
            dh = hs[i] - h[i]
            moved = dh * jnp.where(dh > 0, cs[i], c[i]) + (cs[i] - c[i])
            f.append(w[i] * dh)
            g.append(w[i] * moved)
        fb, gb = back(f), back(g)
        f = [a - b for a, b in zip(f, fb)]
        g = [a - b for a, b in zip(g, gb)]
        flow = f if flow is None else [a + b for a, b in zip(flow, f)]
        salt = g if salt is None else [a + b for a, b in zip(salt, g)]
    return flow, salt


def get(ref, at, n):
    return [ref[at, 8 * m : 8 * m + 8, :] for m in range(n)]


def put(ref, at, values):
    for m, x in enumerate(values):
        ref[at, 8 * m : 8 * m + 8, :] = x


def sweep(first, count, body, carry, unroll=None):
    unroll = unroll or UNROLL
    turns = count // unroll

    def turn(t, carry):
        for i in range(unroll):
            carry = body(first + t * unroll + i, carry)
        return carry

    carry = lax.fori_loop(0, turns, turn, carry)
    for i in range(turns * unroll, count):
        carry = body(first + i, carry)
    return carry


def zeros(n):
    return [jnp.zeros((8, 128), F32)] * n


def scaled(t):
    return [HEAD_SCALE * x for x in t]


def tilt():
    size = 0.5 * HEAD_SCALE * density_slope
    return jnp.where(lanes((8, 128)) < 64, size, -size).astype(F32)


def unfold(a, rim, high, low, start, ext, stage):
    inner = jnp.bitwise_and(lanes((8, 128)), 63)

    def eight(q, pair, part):
        block = start + pair
        first = 108 * part
        for m in range(18):
            stage[m, 0:4, :] = high[block, first + 6 * m : first + 6 * m + 4, :]
            stage[m, 4:8, :] = low[block, first + 6 * m + 2 : first + 6 * m + 6, :]
            stage[m, 8:10, :] = high[block, first + 6 * m + 4 : first + 6 * m + 6, :]
            stage[m, 14:16, :] = low[block, first + 6 * m : first + 6 * m + 2, :]
        for h in range(2):
            for e in range(4):
                ext[q * 8 + 4 * h + e, 0:24, :] = rim[a * 48 + q * 8 + 4 * h + e, 0:24, :]
            for j in range(J):
                m = (h * J + j) * 3
                for i in range(2):
                    x = [stage[m + p, 8 * i : 8 * i + 8, :] for p in range(3)]
                    x.append(fourth(x, inner))
                    at = 24 * (i + 1) + 8 * j
                    for e in range(4):
                        ext[q * 8 + 4 * h + e, at : at + 8, :] = x[e]

    def sixteen(pair, _):
        for part in range(2):
            eight(2 * pair + part, pair, part)
        return 0

    stage[...] = jnp.zeros(stage.shape, F32)
    lax.fori_loop(0, ext.shape[0] // 16, sixteen, 0)


def weights(rim, high, low, wx, wy, vv, fx, fy, base, head, cond, stage):
    unfold(2, rim, high, low, 0, cond, stage)
    unfold(0, rim, high, low, 3, head, stage)
    steps = head.shape[0]
    n = 3 * J
    lane = lanes((8, 128))
    sub = rows_of((8, 128))
    inner = jnp.bitwise_and(lane, 63)
    gx, gy = lax.axis_index("gx"), lax.axis_index("gy")
    last_x, last_y = lax.axis_size("gx") - 1, lax.axis_size("gy") - 1
    has = lambda there: jnp.where(there, 1.0, 0.0).astype(F32)
    beside = jnp.where(sub < 4, has(gx < last_x), has(gx > 0))
    rows = [jnp.ones((8, 128), F32), beside, beside * jnp.where((sub < 2) | (sub >= 6), 1.0, 0.0)]
    masks = []
    for i in range(3):
        for j in range(J):
            y = column(lane, j)
            in_low = jnp.where(y >= -HALO, has(gy > 0), 0.0)
            in_high = jnp.where(y < 128 + HALO, has(gy < last_y), 0.0)
            masks.append(rows[i] * jnp.where(inner < 48, jnp.where(y < 0, in_low, jnp.where(y < 128, 1.0, in_high)), 0.0))

    def known(at):
        return [jnp.where(m > 0, x, 1.0) for m, x in zip(masks, get(cond, at, n))]

    def one(at, k, inmost=False):
        k_in = swap(k) if inmost else known(at + 1)
        rock = [jnp.sqrt(x) * m for m, x in zip(masks, k)]
        x = [time_step * a * b for a, b in zip(rock, up(rock))]
        y = [time_step * a * b for a, b in zip(rock, nxt(rock))]
        put(wx, at, x)
        put(wy, at, y)
        put(vv, at, [2.0 * a * b / (a + b) for a, b in zip(k, k_in)])
        h = scaled(get(head, at, n))
        x = [w * (a - b) for w, a, b in zip(x, up(h), h)]
        y = [w * (a - b) for w, a, b in zip(y, nxt(h), h)]
        put(fx, at, x)
        put(fy, at, y)
        put(base, at, [a + (b - p) + (c - q) for a, b, p, c, q in zip(h, x, down(x), y, prv(y))])
        return k_in

    one(steps - 1, sweep(0, steps - 1, one, known(0), 4), True)


def prepare(rim, high, low, wx, wy, vv, fx, fy, base, part, side, salt, stage):
    unfold(1, rim, high, low, 0, salt, stage)
    steps = salt.shape[0]
    n = 3 * J
    weigh = tilt()

    def carried(w, f, c, ahead, back):
        g = [p * jnp.where(p > 0, a, b) + q * (a - b) for p, q, a, b in zip(f, w, ahead(c), c)]
        return [a - b for a, b in zip(g, back(g))]

    def one(at, carry, inmost=False):
        c, lift_above = carry
        c_in = swap(c) if inmost else get(salt, at + 1, n)
        lift = [(weigh * b) * (p + q) for b, p, q in zip(get(vv, at, n), c, c_in)]
        x = carried(get(wx, at, n), get(fx, at, n), c, up, down)
        y = carried(get(wy, at, n), get(fy, at, n), c, nxt, prv)
        put(part, at, [a - p + q for a, p, q in zip(get(base, at, n), lift, lift_above)])
        put(side, at, [HEAD_SCALE * porosity * a + (b + d) for a, b, d in zip(c, x, y)])
        return c_in, lift

    one(steps - 1, sweep(0, steps - 1, one, (get(salt, 0, n), zeros(n)), 4), True)


def aquifer(part0, side0, salt0, wx, wy, vv, gathered, leak_high, leak_low, head_to, salt_to, hy, cz, ss, ip, uu, iq, kk, mid, leak, head_out, salt_out, sems):
    steps = salt0.shape[0]
    layers = 2 * steps
    lane = lanes((8, 128))
    inner = jnp.bitwise_and(lane, 63)
    weigh = tilt()

    leak[0:8, :] = gathered[2:10, :]
    leak[0:2, :] += leak_low[6:8, :]
    leak[6:8, :] += leak_high[0:2, :]
    leak[8:12, :] = leak_high[2:6, :]
    leak[8:10, :] += gathered[10:12, :]
    leak[12:16, :] = leak_low[2:6, :]
    leak[14:16, :] += gathered[0:2, :]
    leak[16:18, :] = leak_high[6:8, :]
    leak[18:22, :] = jnp.zeros((4, 768), F32)
    leak[22:24, :] = leak_low[0:2, :]

    def leak_of(term, n):
        out = []
        for m in range(n):
            i, j = m // J, m % J
            y = column(lane, j)
            here = leak[8 * i : 8 * i + 8, 256 * term : 256 * term + 128]
            beside = leak[8 * i : 8 * i + 8, 256 * term + 128 : 256 * term + 256]
            x = jnp.where((y >= 0) & (y < 128), take(here, jnp.clip(y, 0, 127)), take(beside, jnp.bitwise_and(y, 127)))
            out.append(jnp.where(lane < 48, x, 0.0))
        return out

    n = 3 * J
    total, level = leak_of(0, n), scaled(leak_of(1, n))

    def pivots(at, carry):
        p, q, flow = carry
        v = get(vv, at, n)
        inverse = [1.0 / (a + b) for a, b in zip(p, v)]
        u = [a * b for a, b in zip(v, inverse)]
        put(ip, at, inverse)
        put(uu, at, u)
        y = [(a + b) * i for a, b, i in zip(get(part0, at, n), flow, inverse)]
        put(hy, at, y)
        inverse = [1.0 / (a + b) for a, b in zip(q, v)]
        k = [a * b for a, b in zip(v, inverse)]
        put(iq, at, inverse)
        put(kk, at, k)
        return (
            [1.0 + a * (1.0 - b) for a, b in zip(v, u)],
            [HEAD_SCALE * porosity + a * (1.0 - b) for a, b in zip(v, k)],
            [a * b for a, b in zip(v, y)],
        )

    sweep(0, steps, pivots, ([1.0 + x for x in total], [HEAD_SCALE * porosity + HEAD_SCALE * x for x in total], level))
    for place, ref in enumerate((uu, kk)):
        u = get(ref, steps - 1, n)
        put(mid, place, [1.0 / (1.0 - a * b) for a, b in zip(u, swap(u))])

    in_order = [jnp.right_shift((lane + 8 - j) * 21846, 16) for j in range(J)]
    owner = lane + 8 - 3 * jnp.right_shift((lane + 8) * 21846, 16)

    def write(out, at, x):
        for end in range(2):
            y = [take(z, jnp.clip(index, 0, 63) + 64 * end) for z, index in zip(x, in_order)]
            layer = at if end == 0 else layers - 1 - at
            out[layer] = jnp.where(owner == 0, y[0], jnp.where(owner == 1, y[1], y[2]))

    def outward(state, ratio, place, n, out=None):
        y, u = get(state, steps - 1, n), get(ratio, steps - 1, n)
        x = [(a + b * c) * d for a, b, c, d in zip(y, u, swap(y), get(mid, place, n))]
        put(state, steps - 1, x)
        if out is not None:
            write(out, steps - 1, x)

        def back(t, x):
            at = steps - 2 - t
            x = [a + b * c for a, b, c in zip(get(state, at, n), get(ratio, at, n), x)]
            if out is None:
                put(state, at, x)
            else:
                write(out, at, x)
            return x

        sweep(0, steps - 1, back, x, steps - 1)

    for step in range(AQ_ITERS):
        last = step == AQ_ITERS - 1
        n_in = J * (3 if step < 2 else 2)
        n = J * (3 if step == 0 else 1 if last else 2)
        salt = salt0 if step == 0 else cz
        if step > 0:
            def inward(at, carry, n_in=n_in, n=n, inmost=False):
                c, lift_above, flow_above = carry
                c_in = swap(c) if inmost else get(cz, at + 1, n_in)
                v = get(vv, at, n)
                lift = [(weigh * b) * (p + q) for b, p, q in zip(v, c, c_in)]
                h = get(hy, at, n_in)
                flow, moved = sides_of(h, c, get(wx, at, n_in), get(wy, at, n_in))
                y = [
                    (a + b - p + q + r) * i
                    for a, b, p, q, r, i in zip(h, flow, lift, lift_above, flow_above, get(ip, at, n))
                ]
                put(hy, at, y)
                put(ss, at, [HEAD_SCALE * porosity * a + b for a, b in zip(c[:n], moved)])
                return c_in, lift, [a * b for a, b in zip(v, y)]

            carry = sweep(0, steps - 1, inward, (get(cz, 0, n_in), zeros(n), scaled(leak_of(1, n))))
            inward(steps - 1, carry, inmost=True)
        outward(hy, uu, 0, n)

        source = side0 if step == 0 else ss

        def salt_inward(at, carry, n=n, salt=salt, source=source, last=last, inmost=False):
            h, c, carried_above, z_above = carry
            h_in = swap(h) if inmost else get(hy, at + 1, n)
            c_in = swap(c) if inmost else get(salt, at + 1, n)
            v = get(vv, at, n)
            rising = [
                x * (time_step * (a - b) - (time_step * weigh) * (p + q))
                for x, a, b, p, q in zip(v, h_in, h, c_in, c)
            ]
            carried = [r * jnp.where(r > 0, p, q) for r, p, q in zip(rising, c_in, c)]
            z = [
                (s + a - b + y) * i
                for s, a, b, y, i in zip(get(source, at, n), carried, carried_above, z_above, get(iq, at, n))
            ]
            put(cz, at, z)
            if last:
                write(head_out, at, [spread_side * x for x in h])
            return h_in, c_in, carried, [x * y for x, y in zip(v, z)]

        carry = sweep(0, steps - 1, salt_inward, (get(hy, 0, n), get(salt, 0, n), zeros(n), scaled(leak_of(2, n))), 16)
        salt_inward(steps - 1, carry, inmost=True)
        if last:
            head_copy = pltpu.make_async_copy(head_out, head_to, sems.at[0])
            head_copy.start()
        outward(cz, kk, 1, n, salt_out if last else None)
    salt_copy = pltpu.make_async_copy(salt_out, salt_to, sems.at[1])
    salt_copy.start()
    head_copy.wait()
    salt_copy.wait()


def whole(steps):
    return (steps, 24 * J, 128)


def run_weights(rim, high, low):
    steps = rim.shape[0] // 3
    return call(
        weights,
        [whole(steps)] * 6,
        (rim, high, low),
        "weights",
        scratch=[pltpu.VMEM(whole(steps), F32)] * 2 + [pltpu.VMEM((18, 16, 128), F32)],
        micros=4.0,
    )


def run_prepare(rim, high, low, *ready):
    steps = rim.shape[0] // 3
    return call(
        prepare,
        [whole(steps)] * 3,
        (rim, high, low, *ready),
        "prepare",
        scratch=[pltpu.VMEM((18, 16, 128), F32)],
        micros=4.0,
    )


def run_aquifer(*args):
    steps = args[0].shape[0]
    return call(
        aquifer,
        [(2 * steps, 8, 128)] * 2,
        args,
        "aquifer",
        scratch=[pltpu.VMEM(whole(steps), F32)] * 7 + [pltpu.VMEM((2, 24 * J, 128), F32), pltpu.VMEM((24, 768), F32)]
        + [pltpu.VMEM((2 * steps, 8, 128), F32)] * 2
        + [pltpu.SemaphoreType.DMA((2,))],
        keep=(0, 1),
        away=(0, 1),
        micros=20.0,
    )


def local(surf_depth, surf_bed, surf_conv, wet_mask, surf_salt, seabed_leak, seabed_shift, active_count, aq_head, aq_salt, aq_cond):
    shifts = seabed_shift.reshape(-1, 2).T
    counts = active_count.reshape(1, -1)
    steps = aq_head.shape[0] // 2
    args = (surf_depth, surf_bed, surf_conv, wet_mask, surf_salt, seabed_leak, shifts, counts, aq_head, aq_salt, aq_cond)
    rim = (152, 128)
    in_low, in_high, rows_low, rows_high, *args = call(
        pack_inland,
        [rim, rim, (8, 128), (8, 128), *(jax.typeof(x) for x in args)],
        args,
        "pack_inland",
        scratch=[pltpu.SemaphoreType.DMA((11,))],
        raw=range(11),
        micros=3.0,
    )
    aq = args[8:]
    right = shift(in_low, "gy", -1)
    left = shift(in_high, "gy", 1)
    tiles = call(interleave, [(steps // 8, 18, 8, 128)] * 3, aq, "interleave", micros=4.0)
    join_low, join_high = call(join_rims, [(24, 128)] * 2, (right, left, rows_low, rows_high, tiles[0]), "join_rims")
    above = shift(join_low, "gx", -1)
    below = shift(join_high, "gx", 1)
    blocks = 3 * steps // 8
    full, *coast = call(
        pack_coast,
        [(blocks, 18, 8, 128)] + [(blocks // 3, 216, 128)] * 2 + [(blocks // 6, 216, 128)] * 2,
        (*tiles, right, left),
        "pack_coast",
        micros=3.0,
    )
    rims = call(open_tile, [(3 * steps, 8 * J, 128)], (full,), "open_tile", micros=3.0)[0]
    first_low, first_high = behind(coast[:2], above, below)
    first = shift(first_low, "gx", -1), shift(first_high, "gx", 1)
    depth, to_low, to_high, to_low2, to_high2, own = call(
        surface,
        [(128, 128), (32, 384), (32, 384), (16, 384), (16, 384), (16, 768)],
        (*args[:8], right, left, above, below),
        "surface",
        scratch=[pltpu.VMEM((136, 256), F32)] * 2,
        keep=(0,),
        micros=1.5,
    )
    leak_right = shift(to_low, "gy", -1)
    leak_left = shift(to_high, "gy", 1)
    leak_right2 = shift(to_low2, "gy", -2)
    leak_left2 = shift(to_high2, "gy", 2)
    then_low, then_high = behind(coast[2:], leak_right, leak_left, leak_right2, leak_left2, rims)
    then = shift(then_low, "gx", -1), shift(then_high, "gx", 1)
    *links, fx, fy, base = run_weights(rims, *first)
    ready = run_prepare(rims, *then, *links, fx, fy, base)
    gathered, sum_low, sum_high = call(
        sum_inland, [(16, 768), (8, 768), (8, 768)], (own, leak_right, leak_left, leak_right2, leak_left2), "sum_inland"
    )
    leak_high = shift(sum_low, "gx", -1)
    leak_low = shift(sum_high, "gx", 1)
    head, salt = run_aquifer(*ready, *links, gathered, leak_high, leak_low)
    return depth, head, salt


def solution(mesh):
    in_specs = (
        P("gx", "gy"),
        P("gx", "gy"),
        P("gx", "gy"),
        P("gx", "gy"),
        P("gx", "gy"),
        P("gx", "gy"),
        P("gx", "gy", None, None),
        P("gx", "gy", None),
        P(None, "gx", "gy"),
        P(None, "gx", "gy"),
        P(None, "gx", "gy"),
    )
    out_specs = (P("gx", "gy"), P(None, "gx", "gy"), P(None, "gx", "gy"))
    return jax.shard_map(local, mesh=mesh, in_specs=in_specs, out_specs=out_specs, check_vma=False)
```
